32 devices in a mesh: groups: 2 (over y), seq: 8 (over z, x), head: 2 (over core).
Axes of the slice: x: 2, y: 2, z: 4, core: 2. Of those that a mesh axis runs over, the one named last changes fastest.
Arguments:
- queries: bfloat16 [3072, 768], P(('groups', 'seq'), 'head'), parts along dimension 0, may hold values from -6 to 6
- key_input: bfloat16 [3072, 768], P(('groups', 'seq'), 'head'), parts along dimension 0, may hold values from -6 to 6
- value_input: bfloat16 [3072, 768], P(('groups', 'seq'), 'head'), parts along dimension 0, may hold values from -6 to 6
- grad_output: bfloat16 [3072, 768], P(('groups', 'seq'), 'head'), parts along dimension 0, may hold values from -6 to 6
- rand_blocks: int32 [48, 12, 3], P(('groups', 'seq'), 'head'), parts along dimension 0, may hold values from 0 to 23, as said below
- global_pos: int32 [512], P('groups'), parts along dimension 0, may hold values from 0 to 1535, as said below
Outputs:
- attended: bfloat16 [3072, 768], P(('groups', 'seq'), 'head'), parts along dimension 0
- query_grad: bfloat16 [3072, 768], P(('groups', 'seq'), 'head'), parts along dimension 0
- key_grad: bfloat16 [3072, 768], P(('groups', 'seq'), 'head'), parts along dimension 0
- value_grad: bfloat16 [3072, 768], P(('groups', 'seq'), 'head'), parts along dimension 0
The draws below stay inside these ranges and needn't reach their ends.
There are 2 independent parts, one for each index of `groups`. The reference program is written for one: setup_inputs(seed, part) draws one part's arguments, and reference() takes and returns one part's arrays. A program takes and returns all parts, laid end to end along the dimension named above; each array names one. Nothing has to cross between parts.
Inputs may be any that keep to these rules, and one draw needn't show every extreme that they name: `rand_blocks`: entries are block numbers. For each seq shard of 3 query blocks and each group of heads g * 6 to g * 6 + 5, at most 7 of its 54 entries lie in one span of 3 blocks that starts at a multiple of 3, and exactly 7 in some span. `global_pos`: distinct positions; at most 64 of them lie in one span of 192 positions that starts at a multiple of 192, and exactly 64 in some span.
All inputs are finite; a program needn't handle non-finite values.
Results may differ from the reference program's by a relative error of at most 0.017.
Values may be sent and summed in bfloat16 or wider, within the bound.
No kernel may reach another device: no remote copies, remote signals or barrier semaphores. Data moves between devices by JAX's collectives and lax.ppermute only.
A program may use at most 64 MiB of HBM per device.

```python
import math
import jax
import jax.numpy as jnp
from jax import lax

HEADS = 12
HEAD_DIM = 64
BLOCK = 64
RAND = 3
GLOBALS = 256
BLK_DEV = 3
TOK_DEV = 192
NBLK = 24
SEQLEN = 1536
HEADS_DEV = 6
REQ = 54
CAP = 7
GMAX = 64
N_SEQ = 8


def draw_pair(key):
    base_key = jax.random.fold_in(key, 11)
    shape_all = (SEQLEN, HEADS * HEAD_DIM)
    query_f = jnp.clip(jax.random.normal(jax.random.fold_in(base_key, 1), shape_all, jnp.float32), -6.0, 6.0)
    key_f = jnp.clip(jax.random.normal(jax.random.fold_in(base_key, 2), shape_all, jnp.float32), -6.0, 6.0)
    return (query_f, key_f)


def draw_queries(key, part):
    return draw_pair(key)[0].astype(jnp.bfloat16)


def draw_key_input(key, part):
    return draw_pair(key)[1].astype(jnp.bfloat16)


def draw_rand_blocks(key, part):
    candidate_count = N_SEQ * CAP
    head_groups = HEADS // HEADS_DEV
    candidate_holder = jnp.arange(candidate_count, dtype=jnp.int32) // CAP
    popular_block_holder = jax.random.randint(jax.random.fold_in(key, 7), (N_SEQ,), 0, 8) == 0

    def one_list(index):
        local_key = jax.random.fold_in(key, index)
        jitter_priority_score = jax.random.randint(jax.random.fold_in(local_key, 1), (candidate_count,), 0, 4096)
        selected_items = jax.random.randint(jax.random.fold_in(local_key, 2), (), 0, N_SEQ)
        extra_priority_score = jnp.where(candidate_holder == selected_items, 16384, 0) + jnp.where(popular_block_holder[candidate_holder], 8192, 0)
        sorted_order = (jitter_priority_score + extra_priority_score) * candidate_count + jnp.arange(candidate_count, dtype=jnp.int32)
        picked = lax.top_k(sorted_order, REQ)[1]
        within = jax.random.randint(jax.random.fold_in(local_key, 3), (REQ,), 0, BLK_DEV)
        return (candidate_holder[picked] * BLK_DEV + within).astype(jnp.int32)
    block_lists = jax.vmap(one_list)(jnp.arange(N_SEQ * head_groups, dtype=jnp.int32) + 100)
    block_lists = block_lists.reshape(N_SEQ, head_groups, BLK_DEV, HEADS_DEV, RAND).transpose(0, 2, 1, 3, 4)
    return block_lists.reshape(NBLK, HEADS, RAND)


def draw_global_pos(key, part):
    candidate_count = N_SEQ * GMAX
    pool_ids = jnp.arange(candidate_count, dtype=jnp.int32)
    candidate_holder = pool_ids // GMAX
    pool_place = pool_ids % GMAX
    jitter_priority_score = jax.random.randint(jax.random.fold_in(key, 21), (candidate_count,), 0, 4096)
    selected_items = jax.random.randint(jax.random.fold_in(key, 22), (), 0, N_SEQ)
    sorted_order = (jitter_priority_score + jnp.where(candidate_holder == selected_items, 8192, 0)) * candidate_count + pool_ids
    picked = lax.top_k(sorted_order, GLOBALS)[1]
    span_size = TOK_DEV // GMAX
    within = jax.random.randint(jax.random.fold_in(key, 23), (GLOBALS,), 0, span_size)
    return (candidate_holder[picked] * TOK_DEV + pool_place[picked] * span_size + within).astype(jnp.int32)


def levels(rng, shape, split, smallest, top_value):
    def one(dim, shards_of):
        steps = jax.random.uniform(jax.random.fold_in(jax.random.fold_in(rng, 6), dim), (shards_of,), jnp.float32, smallest / len(split), top_value / len(split))
        return jnp.repeat(jnp.exp(steps), shape[dim] // shards_of).reshape((-1,) + (1,) * (len(shape) - dim - 1))

    gain = one(*split[0])
    for cut in split[1:]:
        gain = gain * one(*cut)
    return gain


def normal_values(stream_key, shape, spread, limit, split=(), kind=jnp.bfloat16):
    values = spread * jax.random.normal(stream_key, shape, jnp.float32)
    if split:
        values = values * levels(stream_key, shape, split, -0.22, 0.18)
    return jnp.clip(values, -limit, limit).astype(kind)


def setup_inputs(seed: int = 0, part: int = 0) -> dict:
    keys = jax.random.split(jax.random.key(seed), 7)
    part_keys = jax.random.split(jax.random.fold_in(keys[6], part), 7)
    queries = draw_queries(jax.random.fold_in(jax.random.fold_in(keys[6], part), 71), part)
    key_input = draw_key_input(jax.random.fold_in(jax.random.fold_in(keys[6], part), 71), part)
    value_input = normal_values(part_keys[2], (SEQLEN, HEADS * HEAD_DIM), 1.0, 6.0, ((0, 8), (1, 2)))
    grad_output = normal_values(part_keys[3], (SEQLEN, HEADS * HEAD_DIM), 1.0, 6.0, ((0, 8), (1, 2)))
    rand_blocks = draw_rand_blocks(jax.random.fold_in(jax.random.fold_in(keys[6], part), 71), part)
    global_pos = draw_global_pos(jax.random.fold_in(jax.random.fold_in(keys[6], part), 71), part)
    return dict(queries=queries, key_input=key_input, value_input=value_input, grad_output=grad_output, rand_blocks=rand_blocks, global_pos=global_pos)


MASKED = -1e+30

def rounded(value):
    return lax.optimization_barrier(value.astype(jnp.bfloat16)).astype(jnp.float32)

def attend(query, key_rows, value_rows, visible, global_keys, global_values, grad_out, score_scale):
    query_f = query.astype(jnp.float32)
    keys_f = key_rows.astype(jnp.float32)
    values_f = value_rows.astype(jnp.float32)
    gkeys_f = global_keys.astype(jnp.float32)
    gvalues_f = global_values.astype(jnp.float32)
    grad_f = grad_out.astype(jnp.float32)
    local_score = jnp.einsum('nhqe,nhke->nhqk', query_f, keys_f) * score_scale
    local_score = jnp.where(visible, local_score, MASKED)
    global_score = jnp.einsum('nhqe,hke->nhqk', query_f, gkeys_f) * score_scale
    highest = jnp.maximum(lax.optimization_barrier(jnp.max(local_score, axis=-1, keepdims=True)), lax.optimization_barrier(jnp.max(global_score, axis=-1, keepdims=True)))
    local_exp = jnp.exp(local_score - highest)
    global_exp = jnp.exp(global_score - highest)
    totals = lax.optimization_barrier(jnp.sum(local_exp, axis=-1, keepdims=True)) + lax.optimization_barrier(jnp.sum(global_exp, axis=-1, keepdims=True))
    local_weight = rounded(local_exp / totals)
    global_weight = rounded(global_exp / totals)
    outputs = (jnp.einsum('nhqk,nhke->nhqe', local_weight, values_f) + jnp.einsum('nhqk,hke->nhqe', global_weight, gvalues_f)).astype(jnp.bfloat16)
    local_dp = jnp.einsum('nhqe,nhke->nhqk', grad_f, values_f)
    global_dp = jnp.einsum('nhqe,hke->nhqk', grad_f, gvalues_f)
    delta_sum = lax.optimization_barrier(jnp.sum(local_weight * local_dp, axis=-1, keepdims=True)) + lax.optimization_barrier(jnp.sum(global_weight * global_dp, axis=-1, keepdims=True))
    local_ds = rounded(local_weight * (local_dp - delta_sum) * score_scale)
    global_ds = rounded(global_weight * (global_dp - delta_sum) * score_scale)
    grad_query = (jnp.einsum('nhqk,nhke->nhqe', local_ds, keys_f) + jnp.einsum('nhqk,hke->nhqe', global_ds, gkeys_f)).astype(jnp.bfloat16)
    local_dk = jnp.einsum('nhqk,nhqe->nhke', local_ds, query_f)
    local_dv = jnp.einsum('nhqk,nhqe->nhke', local_weight, grad_f)
    global_dk = jnp.einsum('nhqk,nhqe->hke', global_ds, query_f)
    global_dv = jnp.einsum('nhqk,nhqe->hke', global_weight, grad_f)
    return (outputs, grad_query, local_dk, local_dv, global_dk, global_dv)

def reference(queries, key_input, value_input, grad_output, rand_blocks, global_pos):
    positions = queries.shape[0]
    block_total = positions // BLOCK
    group_size = math.gcd(block_total, 16)
    score_scale = 1.0 / math.sqrt(HEAD_DIM)

    def to_blocks(array):
        return array.reshape(block_total, BLOCK, HEADS, HEAD_DIM).transpose(0, 2, 1, 3)
    query_blocks = to_blocks(queries)
    key_blocks = to_blocks(key_input)
    value_blocks = to_blocks(value_input)
    grad_blocks = to_blocks(grad_output)
    zero_block = jnp.zeros((1, HEADS, BLOCK, HEAD_DIM), queries.dtype)
    key_padded = jnp.concatenate([zero_block, key_blocks, zero_block], axis=0)
    value_padded = jnp.concatenate([zero_block, value_blocks, zero_block], axis=0)
    global_keys = key_input[global_pos].reshape(-1, HEADS, HEAD_DIM).transpose(1, 0, 2)
    global_values = value_input[global_pos].reshape(-1, HEADS, HEAD_DIM).transpose(1, 0, 2)
    head_ids = jnp.arange(HEADS, dtype=jnp.int32)

    def piece(group_index):
        block_ids = group_index * group_size + jnp.arange(group_size, dtype=jnp.int32)
        window_keys = jnp.concatenate([key_padded[block_ids + offset] for offset in range(3)], axis=2)
        window_values = jnp.concatenate([value_padded[block_ids + offset] for offset in range(3)], axis=2)
        selected_items = rand_blocks[block_ids]
        random_keys = key_blocks[selected_items, head_ids[None, :, None]].reshape(group_size, HEADS, RAND * BLOCK, HEAD_DIM)
        random_values = value_blocks[selected_items, head_ids[None, :, None]].reshape(group_size, HEADS, RAND * BLOCK, HEAD_DIM)
        key_rows = jnp.concatenate([window_keys, random_keys], axis=2)
        value_rows = jnp.concatenate([window_values, random_values], axis=2)
        neighbour = block_ids[:, None] + jnp.arange(3, dtype=jnp.int32)[None, :] - 1
        inside = (neighbour >= 0) & (neighbour < block_total)
        visible = jnp.concatenate([jnp.repeat(inside, BLOCK, axis=1), jnp.ones((group_size, RAND * BLOCK), jnp.bool_)], axis=1)[:, None, None, :]
        outputs, grad_query, local_dk, local_dv, global_dk, global_dv = attend(query_blocks[block_ids], key_rows, value_rows, visible, global_keys, global_values, grad_blocks[block_ids], score_scale)
        random_dk = local_dk[:, :, 3 * BLOCK:].reshape(group_size, HEADS, RAND, BLOCK, HEAD_DIM).astype(jnp.bfloat16)
        random_dv = local_dv[:, :, 3 * BLOCK:].reshape(group_size, HEADS, RAND, BLOCK, HEAD_DIM).astype(jnp.bfloat16)
        return (outputs, grad_query, local_dk[:, :, :3 * BLOCK], local_dv[:, :, :3 * BLOCK], random_dk, random_dv, global_dk, global_dv)
    results = lax.map(piece, jnp.arange(block_total // group_size, dtype=jnp.int32))

    def flatten(array):
        return array.reshape((block_total,) + array.shape[2:])
    outputs, grad_query, window_dk, window_dv, random_dk, random_dv = [flatten(item) for item in results[:6]]
    global_dk = lax.optimization_barrier(jnp.sum(results[6], axis=0))
    global_dv = lax.optimization_barrier(jnp.sum(results[7], axis=0))

    def window_sum(window):
        zero_f = jnp.zeros((1, HEADS, BLOCK, HEAD_DIM), jnp.float32)
        middle = window[:, :, BLOCK:2 * BLOCK]
        from_next = jnp.concatenate([window[1:, :, :BLOCK], zero_f], axis=0)
        from_prev = jnp.concatenate([zero_f, window[:-1, :, 2 * BLOCK:]], axis=0)
        return middle + from_next + from_prev

    def random_sum(grads):
        grads_f = lax.optimization_barrier(grads).astype(jnp.float32)
        return jnp.zeros((block_total, HEADS, BLOCK, HEAD_DIM), jnp.float32).at[rand_blocks, head_ids[None, :, None]].add(grads_f)

    def global_rows(grads):
        return jnp.zeros((positions, HEADS, HEAD_DIM), jnp.float32).at[global_pos].add(grads.transpose(1, 0, 2))

    def to_rows(array):
        return array.transpose(0, 2, 1, 3).reshape(positions, HEADS, HEAD_DIM)
    key_total = to_rows(window_sum(window_dk) + random_sum(random_dk)) + global_rows(global_dk)
    value_total = to_rows(window_sum(window_dv) + random_sum(random_dv)) + global_rows(global_dv)
    width_all = HEADS * HEAD_DIM
    return (to_rows(outputs).reshape(positions, width_all), to_rows(grad_query).reshape(positions, width_all), key_total.reshape(positions, width_all).astype(jnp.bfloat16), value_total.reshape(positions, width_all).astype(jnp.bfloat16))
```

```python
import functools
import math

import jax
import jax.numpy as jnp
from jax import lax
from jax.experimental import pallas as pl
from jax.experimental.pallas import tpu as pltpu
from jax.sharding import PartitionSpec as P

HEAD_DIM = 64
BLOCK = 64
RAND = 3


MASKED = -1e30


def with_halo(array, sides, width):
    for axis, dim in sides:
        size, length = (lax.axis_size(axis), array.shape[dim])
        up = [(i, (i + 1) % size) for i in range(size - 1)]
        down = [(j, i) for i, j in up]
        last = lax.slice_in_dim(array, length - width, length, axis=dim)
        initial = lax.slice_in_dim(array, 0, width, axis=dim)
        before = lax.ppermute(last, axis, up)
        after = lax.ppermute(initial, axis, down)
        array = jnp.concatenate([before, array, after], axis=dim)
    return array


def attend_head(
    query, key_rows, value_rows, visible, global_keys, global_values, grad_out, score_scale
):
    local_score = (
        jnp.einsum("nqe,nke->nqk", query, key_rows, preferred_element_type=jnp.float32)
        * score_scale
    )
    local_score = jnp.where(visible, local_score, MASKED)
    global_score = (
        jnp.einsum("nqe,ke->nqk", query, global_keys, preferred_element_type=jnp.float32)
        * score_scale
    )
    highest = jnp.maximum(
        jnp.max(local_score, axis=-1, keepdims=True), jnp.max(global_score, axis=-1, keepdims=True)
    )
    local_exp = jnp.exp(local_score - highest)
    global_exp = jnp.exp(global_score - highest)
    totals = jnp.sum(local_exp, axis=-1, keepdims=True) + jnp.sum(
        global_exp, axis=-1, keepdims=True
    )
    local_weight = (local_exp / totals).astype(jnp.bfloat16)
    global_weight = (global_exp / totals).astype(jnp.bfloat16)
    outputs = (
        jnp.einsum("nqk,nke->nqe", local_weight, value_rows, preferred_element_type=jnp.float32)
        + jnp.einsum(
            "nqk,ke->nqe", global_weight, global_values, preferred_element_type=jnp.float32
        )
    ).astype(jnp.bfloat16)
    local_dp = jnp.einsum("nqe,nke->nqk", grad_out, value_rows, preferred_element_type=jnp.float32)
    global_dp = jnp.einsum(
        "nqe,ke->nqk", grad_out, global_values, preferred_element_type=jnp.float32
    )
    local_wf = local_weight.astype(jnp.float32)
    global_wf = global_weight.astype(jnp.float32)
    delta_sum = jnp.sum(local_wf * local_dp, axis=-1, keepdims=True) + jnp.sum(
        global_wf * global_dp, axis=-1, keepdims=True
    )
    local_ds = (local_wf * (local_dp - delta_sum) * score_scale).astype(jnp.bfloat16)
    global_ds = (global_wf * (global_dp - delta_sum) * score_scale).astype(jnp.bfloat16)
    grad_query = (
        jnp.einsum("nqk,nke->nqe", local_ds, key_rows, preferred_element_type=jnp.float32)
        + jnp.einsum("nqk,ke->nqe", global_ds, global_keys, preferred_element_type=jnp.float32)
    ).astype(jnp.bfloat16)
    local_dk = jnp.einsum("nqk,nqe->nke", local_ds, query, preferred_element_type=jnp.float32)
    local_dv = jnp.einsum(
        "nqk,nqe->nke", local_weight, grad_out, preferred_element_type=jnp.float32
    )
    global_dk = jnp.einsum("nqk,nqe->ke", global_ds, query, preferred_element_type=jnp.float32)
    global_dv = jnp.einsum(
        "nqk,nqe->ke", global_weight, grad_out, preferred_element_type=jnp.float32
    )
    return (outputs, grad_query, local_dk, local_dv, global_dk, global_dv, local_ds, local_weight)


def sparse_body(queries, key_input, value_input, grad_output, rand_blocks, global_pos):
    tokens = queries.shape[0]
    blocks = tokens // BLOCK
    head_count = queries.shape[1] // HEAD_DIM
    pair_width = 2 * HEAD_DIM
    shards = lax.axis_size("seq")
    own_index = lax.axis_index("seq")
    first_row = own_index * tokens
    score_scale = 1.0 / math.sqrt(HEAD_DIM)
    packed_kv = jnp.concatenate(
        (
            key_input.reshape(tokens, head_count, HEAD_DIM),
            value_input.reshape(tokens, head_count, HEAD_DIM),
        ),
        axis=2,
    )
    padded = with_halo(packed_kv, (("seq", 0),), BLOCK)
    window_kv = jnp.concatenate(
        [
            padded[offset * BLOCK : offset * BLOCK + tokens].reshape(
                blocks, BLOCK, head_count, pair_width
            )
            for offset in range(3)
        ],
        axis=1,
    ).transpose(2, 0, 1, 3)
    request_block = rand_blocks.reshape(-1)
    requests = request_block.shape[0]
    request_ids = jnp.arange(requests, dtype=jnp.int32)
    request_head = request_ids // RAND % head_count
    owner_shard = request_block // blocks
    capacity = max(2, (requests + shards - 1) // shards)
    slots_all = shards * capacity
    earlier = (owner_shard[:, None] == owner_shard[None, :]) & (
        request_ids[None, :] < request_ids[:, None]
    )
    slot_rank = jnp.sum(earlier.astype(jnp.int32), axis=1)
    request_slot = owner_shard * capacity + slot_rank
    slot_match = request_slot[None, :] == jnp.arange(slots_all, dtype=jnp.int32)[:, None]
    slot_used = jnp.any(slot_match, axis=1)
    slot_source = jnp.sum(jnp.where(slot_match, request_ids[None, :], 0), axis=1)
    request_code = request_block % blocks * head_count + request_head
    wanted = jnp.where(slot_used, jnp.take(request_code, slot_source), -1).reshape(shards, capacity)
    block_table = (
        packed_kv.reshape(blocks, BLOCK, head_count, pair_width)
        .transpose(0, 2, 1, 3)
        .reshape(blocks * head_count, BLOCK, pair_width)
    )
    asked_codes = lax.all_to_all(wanted, "seq", split_axis=0, concat_axis=0, tiled=True)
    picked = jnp.take(block_table, jnp.maximum(asked_codes, 0), axis=0)
    fetched, asked_codes = (
        lax.all_to_all(picked, "seq", split_axis=0, concat_axis=0, tiled=True),
        asked_codes,
    )
    random_kv = jnp.take(fetched.reshape(slots_all, BLOCK, pair_width), request_slot, axis=0)
    random_kv = random_kv.reshape(blocks, head_count, RAND * BLOCK, pair_width).transpose(
        1, 0, 2, 3
    )
    local_kv = jnp.concatenate((window_kv, random_kv), axis=2)
    block_ids = own_index * blocks + jnp.arange(blocks, dtype=jnp.int32)
    neighbour = block_ids[:, None] + jnp.arange(3, dtype=jnp.int32)[None, :] - 1
    inside = (neighbour >= 0) & (neighbour < blocks * shards)
    visible = jnp.concatenate(
        (jnp.repeat(inside, BLOCK, axis=1), jnp.ones((blocks, RAND * BLOCK), jnp.bool_)), axis=1
    )[:, None, :]
    global_count = global_pos.shape[0]
    global_ids = jnp.arange(global_count, dtype=jnp.int32)
    row_ids = jnp.arange(tokens, dtype=jnp.int32)
    flat_kv = packed_kv.reshape(tokens, head_count * pair_width)
    row_match = global_pos[:, None] == first_row + row_ids[None, :]
    partial_rows = jnp.dot(
        row_match.astype(jnp.bfloat16), flat_kv, preferred_element_type=jnp.float32
    )
    global_kv = lax.psum(partial_rows, "seq").astype(jnp.bfloat16)
    global_kv = global_kv.reshape(global_count, head_count, pair_width).transpose(1, 0, 2)

    def heads_first(array):
        return array.reshape(blocks, BLOCK, head_count, HEAD_DIM).transpose(2, 0, 1, 3)

    query_heads = heads_first(queries)
    grad_heads = heads_first(grad_output)

    def one_head(operands):
        query, local_pair, global_pair, grad_out = operands
        return attend_head(
            query,
            local_pair[..., :HEAD_DIM],
            local_pair[..., HEAD_DIM:],
            visible,
            global_pair[:, :HEAD_DIM],
            global_pair[:, HEAD_DIM:],
            grad_out,
            score_scale,
        )

    outputs, grad_query, local_dk, local_dv, global_dk, global_dv, local_ds, local_weight = lax.map(
        one_head, (query_heads, local_kv, global_kv, grad_heads)
    )

    def rows_last(array):
        return array.transpose(1, 2, 0, 3).reshape(tokens, head_count * HEAD_DIM)

    local_grad = jnp.concatenate((local_dk, local_dv), axis=3)
    window_grad = local_grad[:, :, : 3 * BLOCK].transpose(1, 2, 0, 3)
    spread = sum(
        (
            jnp.pad(
                window_grad[:, offset * BLOCK : (offset + 1) * BLOCK].reshape(
                    tokens, head_count, pair_width
                ),
                ((offset * BLOCK, (2 - offset) * BLOCK), (0, 0), (0, 0)),
            )
            for offset in range(3)
        )
    )
    rim_pair = jnp.concatenate((spread[:BLOCK], spread[-BLOCK:]), axis=0)
    rim_in = with_halo(rim_pair.astype(jnp.bfloat16), (("seq", 0),), BLOCK).astype(rim_pair.dtype)
    window_total = (
        spread[BLOCK:-BLOCK]
        + jnp.pad(rim_in[:BLOCK], ((0, tokens - BLOCK), (0, 0), (0, 0)))
        + jnp.pad(rim_in[-BLOCK:], ((tokens - BLOCK, 0), (0, 0), (0, 0)))
    )
    random_grad = local_grad[:, :, 3 * BLOCK :].reshape(head_count, blocks, RAND, BLOCK, pair_width)
    random_grad = (
        random_grad.transpose(1, 0, 2, 3, 4)
        .reshape(requests, BLOCK, pair_width)
        .astype(jnp.bfloat16)
    )
    outgoing = jnp.where(slot_used[:, None, None], jnp.take(random_grad, slot_source, axis=0), 0)
    returned = lax.all_to_all(
        outgoing.reshape(shards, capacity, BLOCK, pair_width),
        "seq",
        split_axis=0,
        concat_axis=0,
        tiled=True,
    )
    target = (
        asked_codes.reshape(-1)[None, :]
        == jnp.arange(blocks * head_count, dtype=jnp.int32)[:, None]
    ).astype(jnp.bfloat16)
    random_total = jnp.dot(
        target, returned.reshape(slots_all, BLOCK * pair_width), preferred_element_type=jnp.float32
    )
    random_total = (
        random_total.reshape(blocks, head_count, BLOCK, pair_width)
        .transpose(0, 2, 1, 3)
        .reshape(tokens, head_count, pair_width)
    )
    global_grad = (
        jnp.concatenate((global_dk, global_dv), axis=2)
        .transpose(1, 0, 2)
        .reshape(global_count, head_count * pair_width)
    )
    global_total = lax.psum(global_grad, "seq")
    row_source = jnp.sum(jnp.where(row_match, global_ids[:, None], 0), axis=0)
    row_used = jnp.any(row_match, axis=0)
    global_rows = jnp.where(row_used[:, None], jnp.take(global_total, row_source, axis=0), 0.0)
    grand_total = window_total + random_total + global_rows.reshape(tokens, head_count, pair_width)
    key_rows_out = (
        grand_total[..., :HEAD_DIM].reshape(tokens, head_count * HEAD_DIM).astype(jnp.bfloat16)
    )
    value_rows_out = (
        grand_total[..., HEAD_DIM:].reshape(tokens, head_count * HEAD_DIM).astype(jnp.bfloat16)
    )
    return (rows_last(outputs), rows_last(grad_query), key_rows_out, value_rows_out)


DENSE_ROWS = 4096
VMEM_BYTES = 48 * 1024 * 1024


def dot(left, right, left_dim, right_dim):
    return lax.dot_general(
        left,
        right,
        (((left_dim,), (right_dim,)), ((), ())),
        preferred_element_type=jnp.float32,
    )


def pack_kernel(first_ref, second_ref, packed_ref):
    heads = first_ref.shape[1] // HEAD_DIM
    for head in range(heads):
        cols = slice(head * HEAD_DIM, (head + 1) * HEAD_DIM)
        packed_ref[:, 2 * head * HEAD_DIM : 2 * (head + 1) * HEAD_DIM] = jnp.concatenate(
            (first_ref[:, cols], second_ref[:, cols]), axis=1
        )


def rows_kernel(query_ref, grad_ref, rows_ref):
    heads, rows, _ = rows_ref.shape
    zeros = jnp.zeros((BLOCK, HEAD_DIM), jnp.bfloat16)
    for head in range(heads):
        cols = slice(head * HEAD_DIM, (head + 1) * HEAD_DIM)
        for block in range(rows // (2 * BLOCK)):
            at = slice(block * BLOCK, (block + 1) * BLOCK)
            query = query_ref[at, cols] * jnp.bfloat16(1.0 / math.sqrt(HEAD_DIM))
            base = 2 * block * BLOCK
            rows_ref[head, base : base + BLOCK, :] = jnp.concatenate((query, zeros), axis=1)
            rows_ref[head, base + BLOCK : base + 2 * BLOCK, :] = jnp.concatenate(
                (zeros, grad_ref[at, cols]), axis=1
            )


def unpack_kernel(*refs):
    *packed_refs, first_ref, second_ref = refs
    heads = first_ref.shape[1] // HEAD_DIM
    for head in range(heads):
        wide = slice(2 * head * HEAD_DIM, 2 * (head + 1) * HEAD_DIM)
        total = packed_refs[0][:, wide].astype(jnp.float32)
        for ref in packed_refs[1:]:
            total = total + ref[:, wide].astype(jnp.float32)
        total = total.astype(jnp.bfloat16)
        cols = slice(head * HEAD_DIM, (head + 1) * HEAD_DIM)
        first_ref[:, cols] = total[:, :HEAD_DIM]
        second_ref[:, cols] = total[:, HEAD_DIM:]


def shard_of(own, steps, mate, lines):
    line_pos = lax.rem(own // 2 + steps + lines, lines)
    side = own % 2
    return 2 * line_pos + (1 - side if mate else side)


def attend_kernel(shards, rand_ref, pos_row_ref, pos_col_ref, rows_ref, *refs):
    pieces = refs[:shards]
    packed_ref = refs[shards]
    chunks = refs[shards + 1 : 2 * shards + 1]
    kv, acc, global_kv, global_acc, sems = refs[2 * shards + 1 :]
    tokens = packed_ref.shape[0]
    blocks = tokens // BLOCK
    heads = rows_ref.shape[0]
    global_count = pos_row_ref.shape[1]
    lines = shards // 2
    own = lax.axis_index("seq")

    def rows_at(shard):
        return pl.ds(pl.multiple_of(shard * tokens, BLOCK), tokens)

    copies = []
    for slot in range(shards):
        source = shard_of(own, -(slot % lines), slot >= lines, lines)
        copies.append(
            pltpu.make_async_copy(pieces[slot], kv.at[rows_at(source)], sems.at[slot])
        )
    for copy in copies:
        copy.start()
    acc[...] = jnp.zeros_like(acc)
    position = lax.broadcasted_iota(jnp.int32, (global_count, shards * tokens), 1)
    pick = (position == pos_col_ref[...]).astype(jnp.bfloat16)
    for copy in copies:
        copy.wait()
    global_kv[...] = dot(pick, kv[...], 1, 0).astype(jnp.bfloat16)
    lane = lax.broadcasted_iota(jnp.int32, (BLOCK, 6 * BLOCK), 1)
    half = lax.broadcasted_iota(jnp.int32, (BLOCK, 2 * HEAD_DIM), 1) < HEAD_DIM

    def one_head(head, carry):
        cols = pl.ds(pl.multiple_of(head * 2 * HEAD_DIM, 2 * HEAD_DIM), 2 * HEAD_DIM)
        gkv = global_kv[:, cols]
        rows = rows_ref[head]
        global_dots = dot(rows, gkv, 1, 1)
        global_sides = []
        for block in range(blocks):
            here = own * blocks + block
            places = [
                jnp.maximum(here - 1, 0),
                here,
                jnp.minimum(here + 1, shards * blocks - 1),
            ] + [rand_ref[(block * heads + head) * RAND + r] for r in range(RAND)]
            places = [pl.ds(pl.multiple_of(p * BLOCK, BLOCK), BLOCK) for p in places]
            local_kv = jnp.concatenate([kv[p, cols] for p in places], axis=0)
            base = 2 * block * BLOCK
            both = rows[base : base + 2 * BLOCK]
            local_dots = dot(both, local_kv, 1, 1)
            score, dp = local_dots[:BLOCK], local_dots[BLOCK:]
            if block == 0:
                score = jnp.where((lane < BLOCK) & (here == 0), MASKED, score)
            if block == blocks - 1:
                outside = (lane >= 2 * BLOCK) & (lane < 3 * BLOCK)
                score = jnp.where(outside & (here == shards * blocks - 1), MASKED, score)
            global_score = global_dots[base : base + BLOCK]
            global_dp = global_dots[base + BLOCK : base + 2 * BLOCK]
            highest = jnp.maximum(
                jnp.max(score, axis=1, keepdims=True),
                jnp.max(global_score, axis=1, keepdims=True),
            )
            local_exp = jnp.exp(score - highest)
            global_exp = jnp.exp(global_score - highest)
            inverse = 1.0 / (
                jnp.sum(local_exp, axis=1, keepdims=True)
                + jnp.sum(global_exp, axis=1, keepdims=True)
            )
            local_weight = (local_exp * inverse).astype(jnp.bfloat16)
            global_weight = (global_exp * inverse).astype(jnp.bfloat16)
            local_wf = local_weight.astype(jnp.float32)
            global_wf = global_weight.astype(jnp.float32)
            delta = jnp.sum(local_wf * dp, axis=1, keepdims=True) + jnp.sum(
                global_wf * global_dp, axis=1, keepdims=True
            )
            local_ds = (local_wf * (dp - delta)).astype(jnp.bfloat16)
            global_ds = (global_wf * (global_dp - delta)).astype(jnp.bfloat16)
            local_side = jnp.concatenate((local_ds, local_weight), axis=0)
            global_side = jnp.concatenate((global_ds, global_weight), axis=0)
            global_sides.append(global_side)
            result = dot(local_side, local_kv, 1, 0) + dot(global_side, gkv, 1, 0)
            packed_ref[block * BLOCK : (block + 1) * BLOCK, cols] = jnp.where(
                half, result[:BLOCK] * (1.0 / math.sqrt(HEAD_DIM)), result[BLOCK:]
            ).astype(jnp.bfloat16)
            local_grad = dot(local_side, both, 0, 0)
            for i, place in enumerate(places):
                acc[place, cols] += local_grad[i * BLOCK : (i + 1) * BLOCK]
        global_acc[:, cols] = dot(jnp.concatenate(global_sides, axis=0), rows, 0, 0).astype(
            jnp.bfloat16
        )
        return carry

    lax.fori_loop(0, heads, one_head, 0)
    for slot in range(shards):
        target = shard_of(own, slot % lines, slot >= lines, lines)
        position = target * tokens + lax.broadcasted_iota(jnp.int32, (tokens, global_count), 0)
        spread = (position == pos_row_ref[...]).astype(jnp.bfloat16)
        chunks[slot][...] = (
            acc[rows_at(target)] + dot(spread, global_acc[...], 1, 0)
        ).astype(jnp.bfloat16)


def dense_body(queries, key_input, value_input, grad_output, rand_blocks, global_pos):
    tokens, width = queries.shape
    heads = width // HEAD_DIM
    shards = lax.axis_size("seq")
    lines = shards // 2
    global_count = global_pos.shape[0]
    bf16 = jnp.bfloat16
    params = pltpu.CompilerParams(vmem_limit_bytes=VMEM_BYTES)
    wide = jax.ShapeDtypeStruct((tokens, 2 * width), bf16)
    narrow = jax.ShapeDtypeStruct((tokens, width), bf16)

    def along(array, steps):
        pairs = [(s, (s // 2 + steps) % lines * 2 + s % 2) for s in range(shards)]
        return lax.ppermute(array, "seq", pairs)

    def across(array):
        return lax.ppermute(array, "seq", [(s, s ^ 1) for s in range(shards)])

    def pack(first, second):
        return pl.pallas_call(pack_kernel, out_shape=wide, compiler_params=params)(first, second)

    def unpack(*packed):
        return pl.pallas_call(unpack_kernel, out_shape=(narrow, narrow), compiler_params=params)(
            *packed
        )

    near_first = sorted(range(1, lines), key=lambda k: min(k, lines - k))
    kv = pack(key_input, value_input)
    own_line = [kv] + [None] * (lines - 1)
    mate_line = [across(kv)] + [None] * (lines - 1)
    for steps in near_first:
        own_line[steps] = along(kv, steps)
    for steps in near_first:
        mate_line[steps] = across(own_line[steps])
    rows = pl.pallas_call(
        rows_kernel,
        out_shape=jax.ShapeDtypeStruct((heads, 2 * tokens, 2 * HEAD_DIM), bf16),
        compiler_params=params,
        cost_estimate=pl.CostEstimate(flops=0, bytes_accessed=6 * tokens * width, transcendentals=0),
    )(queries, grad_output)
    vmem = pl.BlockSpec(memory_space=pltpu.VMEM)
    packed, *chunks = pl.pallas_call(
        functools.partial(attend_kernel, shards),
        out_shape=(wide,) * (shards + 1),
        in_specs=[pl.BlockSpec(memory_space=pltpu.SMEM)]
        + [vmem] * 3
        + [pl.BlockSpec(memory_space=pl.ANY)] * shards,
        out_specs=(vmem,) * (shards + 1),
        scratch_shapes=[
            pltpu.VMEM((shards * tokens, 2 * width), bf16),
            pltpu.VMEM((shards * tokens, 2 * width), jnp.float32),
            pltpu.VMEM((global_count, 2 * width), bf16),
            pltpu.VMEM((global_count, 2 * width), bf16),
            pltpu.SemaphoreType.DMA((shards,)),
        ],
        compiler_params=params,
    )(
        rand_blocks.reshape(-1),
        global_pos.reshape(1, -1),
        global_pos.reshape(-1, 1),
        rows,
        *own_line,
        *mate_line,
    )
    far_first = near_first[::-1]
    from_mate = {steps: across(chunks[lines + steps]) for steps in far_first + [0]}
    sent = [
        along(
            (chunks[steps].astype(jnp.float32) + from_mate[steps].astype(jnp.float32)).astype(bf16),
            steps,
        )
        for steps in far_first
    ]
    query_grad, attended = unpack(packed)
    key_grad, value_grad = unpack(chunks[0], from_mate[0], *sent)
    return attended, query_grad, key_grad, value_grad


def body(queries, *others):
    shards = lax.axis_size("seq")
    if shards % 2 == 0 and shards * queries.shape[0] <= DENSE_ROWS:
        return dense_body(queries, *others)
    return sparse_body(queries, *others)


def solution(mesh):
    in_specs = (
        P(("groups", "seq"), "head"),
        P(("groups", "seq"), "head"),
        P(("groups", "seq"), "head"),
        P(("groups", "seq"), "head"),
        P(("groups", "seq"), "head", None),
        P("groups"),
    )
    out_specs = (
        P(("groups", "seq"), "head"),
        P(("groups", "seq"), "head"),
        P(("groups", "seq"), "head"),
        P(("groups", "seq"), "head"),
    )
    return jax.shard_map(body, mesh=mesh, in_specs=in_specs, out_specs=out_specs, check_vma=False)
```

```python
import math

import jax
import jax.numpy as jnp
from jax import lax
from jax.experimental import pallas as pl
from jax.experimental.pallas import tpu as pltpu
from jax.sharding import PartitionSpec as P

HEAD_DIM = 64
BLOCK = 64
RAND = 3


MASKED = -1e30


def with_halo(array, sides, width):
    for axis, dim in sides:
        size, length = (lax.axis_size(axis), array.shape[dim])
        up = [(i, (i + 1) % size) for i in range(size - 1)]
        down = [(j, i) for i, j in up]
        last = lax.slice_in_dim(array, length - width, length, axis=dim)
        initial = lax.slice_in_dim(array, 0, width, axis=dim)
        before = lax.ppermute(last, axis, up)
        after = lax.ppermute(initial, axis, down)
        array = jnp.concatenate([before, array, after], axis=dim)
    return array


def attend_head(
    query, key_rows, value_rows, visible, global_keys, global_values, grad_out, score_scale
):
    local_score = (
        jnp.einsum("nqe,nke->nqk", query, key_rows, preferred_element_type=jnp.float32)
        * score_scale
    )
    local_score = jnp.where(visible, local_score, MASKED)
    global_score = (
        jnp.einsum("nqe,ke->nqk", query, global_keys, preferred_element_type=jnp.float32)
        * score_scale
    )
    highest = jnp.maximum(
        jnp.max(local_score, axis=-1, keepdims=True), jnp.max(global_score, axis=-1, keepdims=True)
    )
    local_exp = jnp.exp(local_score - highest)
    global_exp = jnp.exp(global_score - highest)
    totals = jnp.sum(local_exp, axis=-1, keepdims=True) + jnp.sum(
        global_exp, axis=-1, keepdims=True
    )
    local_weight = (local_exp / totals).astype(jnp.bfloat16)
    global_weight = (global_exp / totals).astype(jnp.bfloat16)
    outputs = (
        jnp.einsum("nqk,nke->nqe", local_weight, value_rows, preferred_element_type=jnp.float32)
        + jnp.einsum(
            "nqk,ke->nqe", global_weight, global_values, preferred_element_type=jnp.float32
        )
    ).astype(jnp.bfloat16)
    local_dp = jnp.einsum("nqe,nke->nqk", grad_out, value_rows, preferred_element_type=jnp.float32)
    global_dp = jnp.einsum(
        "nqe,ke->nqk", grad_out, global_values, preferred_element_type=jnp.float32
    )
    local_wf = local_weight.astype(jnp.float32)
    global_wf = global_weight.astype(jnp.float32)
    delta_sum = jnp.sum(local_wf * local_dp, axis=-1, keepdims=True) + jnp.sum(
        global_wf * global_dp, axis=-1, keepdims=True
    )
    local_ds = (local_wf * (local_dp - delta_sum) * score_scale).astype(jnp.bfloat16)
    global_ds = (global_wf * (global_dp - delta_sum) * score_scale).astype(jnp.bfloat16)
    grad_query = (
        jnp.einsum("nqk,nke->nqe", local_ds, key_rows, preferred_element_type=jnp.float32)
        + jnp.einsum("nqk,ke->nqe", global_ds, global_keys, preferred_element_type=jnp.float32)
    ).astype(jnp.bfloat16)
    local_dk = jnp.einsum("nqk,nqe->nke", local_ds, query, preferred_element_type=jnp.float32)
    local_dv = jnp.einsum(
        "nqk,nqe->nke", local_weight, grad_out, preferred_element_type=jnp.float32
    )
    global_dk = jnp.einsum("nqk,nqe->ke", global_ds, query, preferred_element_type=jnp.float32)
    global_dv = jnp.einsum(
        "nqk,nqe->ke", global_weight, grad_out, preferred_element_type=jnp.float32
    )
    return (outputs, grad_query, local_dk, local_dv, global_dk, global_dv, local_ds, local_weight)


def sparse_body(queries, key_input, value_input, grad_output, rand_blocks, global_pos):
    tokens = queries.shape[0]
    blocks = tokens // BLOCK
    head_count = queries.shape[1] // HEAD_DIM
    pair_width = 2 * HEAD_DIM
    shards = lax.axis_size("seq")
    own_index = lax.axis_index("seq")
    first_row = own_index * tokens
    score_scale = 1.0 / math.sqrt(HEAD_DIM)
    packed_kv = jnp.concatenate(
        (
            key_input.reshape(tokens, head_count, HEAD_DIM),
            value_input.reshape(tokens, head_count, HEAD_DIM),
        ),
        axis=2,
    )
    padded = with_halo(packed_kv, (("seq", 0),), BLOCK)
    window_kv = jnp.concatenate(
        [
            padded[offset * BLOCK : offset * BLOCK + tokens].reshape(
                blocks, BLOCK, head_count, pair_width
            )
            for offset in range(3)
        ],
        axis=1,
    ).transpose(2, 0, 1, 3)
    request_block = rand_blocks.reshape(-1)
    requests = request_block.shape[0]
    request_ids = jnp.arange(requests, dtype=jnp.int32)
    request_head = request_ids // RAND % head_count
    owner_shard = request_block // blocks
    capacity = max(2, (requests + shards - 1) // shards)
    slots_all = shards * capacity
    earlier = (owner_shard[:, None] == owner_shard[None, :]) & (
        request_ids[None, :] < request_ids[:, None]
    )
    slot_rank = jnp.sum(earlier.astype(jnp.int32), axis=1)
    request_slot = owner_shard * capacity + slot_rank
    slot_match = request_slot[None, :] == jnp.arange(slots_all, dtype=jnp.int32)[:, None]
    slot_used = jnp.any(slot_match, axis=1)
    slot_source = jnp.sum(jnp.where(slot_match, request_ids[None, :], 0), axis=1)
    request_code = request_block % blocks * head_count + request_head
    wanted = jnp.where(slot_used, jnp.take(request_code, slot_source), -1).reshape(shards, capacity)
    block_table = (
        packed_kv.reshape(blocks, BLOCK, head_count, pair_width)
        .transpose(0, 2, 1, 3)
        .reshape(blocks * head_count, BLOCK, pair_width)
    )
    asked_codes = lax.all_to_all(wanted, "seq", split_axis=0, concat_axis=0, tiled=True)
    picked = jnp.take(block_table, jnp.maximum(asked_codes, 0), axis=0)
    fetched, asked_codes = (
        lax.all_to_all(picked, "seq", split_axis=0, concat_axis=0, tiled=True),
        asked_codes,
    )
    random_kv = jnp.take(fetched.reshape(slots_all, BLOCK, pair_width), request_slot, axis=0)
    random_kv = random_kv.reshape(blocks, head_count, RAND * BLOCK, pair_width).transpose(
        1, 0, 2, 3
    )
    local_kv = jnp.concatenate((window_kv, random_kv), axis=2)
    block_ids = own_index * blocks + jnp.arange(blocks, dtype=jnp.int32)
    neighbour = block_ids[:, None] + jnp.arange(3, dtype=jnp.int32)[None, :] - 1
    inside = (neighbour >= 0) & (neighbour < blocks * shards)
    visible = jnp.concatenate(
        (jnp.repeat(inside, BLOCK, axis=1), jnp.ones((blocks, RAND * BLOCK), jnp.bool_)), axis=1
    )[:, None, :]
    global_count = global_pos.shape[0]
    global_ids = jnp.arange(global_count, dtype=jnp.int32)
    row_ids = jnp.arange(tokens, dtype=jnp.int32)
    flat_kv = packed_kv.reshape(tokens, head_count * pair_width)
    row_match = global_pos[:, None] == first_row + row_ids[None, :]
    partial_rows = jnp.dot(
        row_match.astype(jnp.bfloat16), flat_kv, preferred_element_type=jnp.float32
    )
    global_kv = lax.psum(partial_rows, "seq").astype(jnp.bfloat16)
    global_kv = global_kv.reshape(global_count, head_count, pair_width).transpose(1, 0, 2)

    def heads_first(array):
        return array.reshape(blocks, BLOCK, head_count, HEAD_DIM).transpose(2, 0, 1, 3)

    query_heads = heads_first(queries)
    grad_heads = heads_first(grad_output)

    def one_head(operands):
        query, local_pair, global_pair, grad_out = operands
        return attend_head(
            query,
            local_pair[..., :HEAD_DIM],
            local_pair[..., HEAD_DIM:],
            visible,
            global_pair[:, :HEAD_DIM],
            global_pair[:, HEAD_DIM:],
            grad_out,
            score_scale,
        )

    outputs, grad_query, local_dk, local_dv, global_dk, global_dv, local_ds, local_weight = lax.map(
        one_head, (query_heads, local_kv, global_kv, grad_heads)
    )

    def rows_last(array):
        return array.transpose(1, 2, 0, 3).reshape(tokens, head_count * HEAD_DIM)

    local_grad = jnp.concatenate((local_dk, local_dv), axis=3)
    window_grad = local_grad[:, :, : 3 * BLOCK].transpose(1, 2, 0, 3)
    spread = sum(
        (
            jnp.pad(
                window_grad[:, offset * BLOCK : (offset + 1) * BLOCK].reshape(
                    tokens, head_count, pair_width
                ),
                ((offset * BLOCK, (2 - offset) * BLOCK), (0, 0), (0, 0)),
            )
            for offset in range(3)
        )
    )
    rim_pair = jnp.concatenate((spread[:BLOCK], spread[-BLOCK:]), axis=0)
    rim_in = with_halo(rim_pair.astype(jnp.bfloat16), (("seq", 0),), BLOCK).astype(rim_pair.dtype)
    window_total = (
        spread[BLOCK:-BLOCK]
        + jnp.pad(rim_in[:BLOCK], ((0, tokens - BLOCK), (0, 0), (0, 0)))
        + jnp.pad(rim_in[-BLOCK:], ((tokens - BLOCK, 0), (0, 0), (0, 0)))
    )
    random_grad = local_grad[:, :, 3 * BLOCK :].reshape(head_count, blocks, RAND, BLOCK, pair_width)
    random_grad = (
        random_grad.transpose(1, 0, 2, 3, 4)
        .reshape(requests, BLOCK, pair_width)
        .astype(jnp.bfloat16)
    )
    outgoing = jnp.where(slot_used[:, None, None], jnp.take(random_grad, slot_source, axis=0), 0)
    returned = lax.all_to_all(
        outgoing.reshape(shards, capacity, BLOCK, pair_width),
        "seq",
        split_axis=0,
        concat_axis=0,
        tiled=True,
    )
    target = (
        asked_codes.reshape(-1)[None, :]
        == jnp.arange(blocks * head_count, dtype=jnp.int32)[:, None]
    ).astype(jnp.bfloat16)
    random_total = jnp.dot(
        target, returned.reshape(slots_all, BLOCK * pair_width), preferred_element_type=jnp.float32
    )
    random_total = (
        random_total.reshape(blocks, head_count, BLOCK, pair_width)
        .transpose(0, 2, 1, 3)
        .reshape(tokens, head_count, pair_width)
    )
    global_grad = (
        jnp.concatenate((global_dk, global_dv), axis=2)
        .transpose(1, 0, 2)
        .reshape(global_count, head_count * pair_width)
    )
    global_total = lax.psum(global_grad, "seq")
    row_source = jnp.sum(jnp.where(row_match, global_ids[:, None], 0), axis=0)
    row_used = jnp.any(row_match, axis=0)
    global_rows = jnp.where(row_used[:, None], jnp.take(global_total, row_source, axis=0), 0.0)
    grand_total = window_total + random_total + global_rows.reshape(tokens, head_count, pair_width)
    key_rows_out = (
        grand_total[..., :HEAD_DIM].reshape(tokens, head_count * HEAD_DIM).astype(jnp.bfloat16)
    )
    value_rows_out = (
        grand_total[..., HEAD_DIM:].reshape(tokens, head_count * HEAD_DIM).astype(jnp.bfloat16)
    )
    return (rows_last(outputs), rows_last(grad_query), key_rows_out, value_rows_out)


WHOLE_ROWS = 4096
EXTRA = 16
VMEM_BYTES = 48 * 1024 * 1024


def dot(left, right, left_dim, right_dim):
    return lax.dot_general(
        left,
        right,
        (((left_dim,), (right_dim,)), ((), ())),
        preferred_element_type=jnp.float32,
    )


def pack_kernel(rand_ref, key_ref, value_ref, query_ref, grad_ref, packed_ref):
    tokens, width = key_ref.shape
    heads = width // HEAD_DIM
    blocks = tokens // BLOCK
    lane = lax.broadcasted_iota(jnp.int32, (EXTRA, 2 * HEAD_DIM), 1)
    for head in range(heads):
        cols = slice(head * HEAD_DIM, (head + 1) * HEAD_DIM)
        packed_ref[head, :tokens, : 2 * HEAD_DIM] = jnp.concatenate(
            (key_ref[:, cols], value_ref[:, cols]), axis=1
        )
        packed_ref[head, :tokens, 2 * HEAD_DIM :] = jnp.concatenate(
            (query_ref[:, cols], grad_ref[:, cols]), axis=1
        )
        listed = jnp.zeros((EXTRA, 2 * HEAD_DIM), jnp.int32)
        for i in range(blocks * RAND):
            entry = rand_ref[(i // RAND * heads + head) * RAND + i % RAND]
            listed = jnp.where(lane == i, entry, listed)
        listed = listed.astype(jnp.float32).astype(jnp.bfloat16)
        packed_ref[head, tokens:, : 2 * HEAD_DIM] = listed
        packed_ref[head, tokens:, 2 * HEAD_DIM :] = jnp.zeros_like(listed)
    for slot in range(heads, packed_ref.shape[0]):
        packed_ref[slot] = jnp.zeros(packed_ref.shape[1:], jnp.bfloat16)


def unpack_kernel(packed_ref, attended_ref, query_ref, key_ref, value_ref):
    heads = key_ref.shape[1] // HEAD_DIM
    for head in range(heads):
        cols = slice(head * HEAD_DIM, (head + 1) * HEAD_DIM)
        for i, ref in enumerate((query_ref, attended_ref, key_ref, value_ref)):
            ref[:, cols] = packed_ref[head, :, i * HEAD_DIM : (i + 1) * HEAD_DIM]


def attend_kernel(
    pos_row_ref, pos_col_ref, x_ref, out_ref, acc, global_kv, global_acc, listed, starts, sem
):
    shards, tokens, _ = out_ref.shape
    stride = x_ref.shape[0] // shards
    blocks = tokens // BLOCK
    global_count = pos_row_ref.shape[1]
    kv_cols = slice(0, 2 * HEAD_DIM)
    rest_cols = slice(2 * HEAD_DIM, 4 * HEAD_DIM)

    for shard in range(shards):
        row = x_ref[shard * stride + tokens : (shard + 1) * stride, kv_cols].astype(jnp.float32)
        passed = jnp.floor((row + 0.5) * (1.0 / blocks))
        first = row * BLOCK + passed * (stride - tokens)
        listed[shard] = first[:8].astype(jnp.int32)
    copy = pltpu.make_async_copy(listed, starts, sem)
    copy.start()
    acc[...] = jnp.zeros_like(acc)
    global_acc[...] = jnp.zeros_like(global_acc)
    place = lax.broadcasted_iota(jnp.int32, (global_count, shards * stride), 1)
    pick = (place == pos_col_ref[...]).astype(jnp.bfloat16)
    global_kv[...] = dot(pick, x_ref[:, kv_cols], 1, 0).astype(jnp.bfloat16)
    copy.wait()
    lane = lax.broadcasted_iota(jnp.int32, (BLOCK, 6 * BLOCK), 1)
    half = lax.broadcasted_iota(jnp.int32, (BLOCK, 2 * HEAD_DIM), 1) < HEAD_DIM
    query_mask = jnp.where(half, 1.0 / math.sqrt(HEAD_DIM), 0.0).astype(jnp.bfloat16)
    grad_mask = jnp.where(half, 0.0, 1.0).astype(jnp.bfloat16)

    def at(start):
        return pl.ds(pl.multiple_of(start, EXTRA), BLOCK)

    def one_shard(shard, carry):
        base = shard * stride
        gkv = global_kv[...]
        rows = []
        for block in range(blocks):
            rest = x_ref[at(base + block * BLOCK), rest_cols]
            rows += [rest * query_mask, rest * grad_mask]
        rows = jnp.concatenate(rows, axis=0)
        global_dots = dot(rows, gkv, 1, 1)
        before = jnp.maximum(shard - 1, 0) * stride + (blocks - 1) * BLOCK
        after = jnp.minimum(shard + 1, shards - 1) * stride
        global_sides = []
        for block in range(blocks):
            places = [
                base + (block - 1) * BLOCK if block else before,
                base + block * BLOCK,
                base + (block + 1) * BLOCK if block < blocks - 1 else after,
            ] + [starts[shard, 0, block * RAND + r] for r in range(RAND)]
            places = [at(p) for p in places]
            local_kv = jnp.concatenate([x_ref[p, kv_cols] for p in places], axis=0)
            top = 2 * block * BLOCK
            both = rows[top : top + 2 * BLOCK]
            local_dots = dot(both, local_kv, 1, 1)
            score, dp = local_dots[:BLOCK], local_dots[BLOCK:]
            if block == 0:
                score = jnp.where((lane < BLOCK) & (shard == 0), MASKED, score)
            if block == blocks - 1:
                outside = (lane >= 2 * BLOCK) & (lane < 3 * BLOCK)
                score = jnp.where(outside & (shard == shards - 1), MASKED, score)
            global_score = global_dots[top : top + BLOCK]
            global_dp = global_dots[top + BLOCK : top + 2 * BLOCK]
            highest = jnp.maximum(
                jnp.max(score, axis=1, keepdims=True),
                jnp.max(global_score, axis=1, keepdims=True),
            )
            local_exp = jnp.exp(score - highest)
            global_exp = jnp.exp(global_score - highest)
            inverse = 1.0 / (
                jnp.sum(local_exp, axis=1, keepdims=True)
                + jnp.sum(global_exp, axis=1, keepdims=True)
            )
            local_weight = (local_exp * inverse).astype(jnp.bfloat16)
            global_weight = (global_exp * inverse).astype(jnp.bfloat16)
            local_wf = local_weight.astype(jnp.float32)
            global_wf = global_weight.astype(jnp.float32)
            delta = jnp.sum(local_wf * dp, axis=1, keepdims=True) + jnp.sum(
                global_wf * global_dp, axis=1, keepdims=True
            )
            local_ds = (local_wf * (dp - delta)).astype(jnp.bfloat16)
            global_ds = (global_wf * (global_dp - delta)).astype(jnp.bfloat16)
            local_side = jnp.concatenate((local_ds, local_weight), axis=0)
            global_side = jnp.concatenate((global_ds, global_weight), axis=0)
            global_sides.append(global_side)
            result = dot(local_side, local_kv, 1, 0) + dot(global_side, gkv, 1, 0)
            out_ref[shard, block * BLOCK : (block + 1) * BLOCK, kv_cols] = jnp.where(
                half, result[:BLOCK] * (1.0 / math.sqrt(HEAD_DIM)), result[BLOCK:]
            ).astype(jnp.bfloat16)
            local_grad = dot(local_side, both, 0, 0)
            for i, spot in enumerate(places):
                acc[spot] += local_grad[i * BLOCK : (i + 1) * BLOCK]
        global_acc[...] += dot(jnp.concatenate(global_sides, axis=0), rows, 0, 0)
        return carry

    lax.fori_loop(0, shards, one_shard, 0)
    global_grad = global_acc[...].astype(jnp.bfloat16)
    for shard in range(shards):
        place = shard * stride + lax.broadcasted_iota(jnp.int32, (tokens, global_count), 0)
        spread = (place == pos_row_ref[...]).astype(jnp.bfloat16)
        out_ref[shard, :, rest_cols] = (
            acc[shard * stride : shard * stride + tokens] + dot(spread, global_grad, 1, 0)
        ).astype(jnp.bfloat16)


def whole_body(queries, key_input, value_input, grad_output, rand_blocks, global_pos):
    tokens, width = queries.shape
    shards = lax.axis_size("seq")
    global_count = global_pos.shape[0]
    stride = tokens + EXTRA
    pair = 2 * HEAD_DIM
    bf16 = jnp.bfloat16
    params = pltpu.CompilerParams(vmem_limit_bytes=VMEM_BYTES)
    narrow = jax.ShapeDtypeStruct((tokens, width), bf16)
    vmem = pl.BlockSpec(memory_space=pltpu.VMEM)
    smem = pl.BlockSpec(memory_space=pltpu.SMEM)
    packed = pl.pallas_call(
        pack_kernel,
        out_shape=jax.ShapeDtypeStruct((shards, stride, 2 * pair), bf16),
        in_specs=[smem] + [vmem] * 4,
        out_specs=vmem,
        compiler_params=params,
    )(rand_blocks.reshape(-1), key_input, value_input, queries, grad_output)
    whole = lax.all_to_all(packed, "seq", split_axis=0, concat_axis=0, tiled=True)
    place = global_pos + global_pos // tokens * EXTRA
    result = pl.pallas_call(
        attend_kernel,
        out_shape=jax.ShapeDtypeStruct((shards, tokens, 2 * pair), bf16),
        in_specs=[vmem] * 3,
        out_specs=vmem,
        scratch_shapes=[
            pltpu.VMEM((shards * stride, pair), jnp.float32),
            pltpu.VMEM((global_count, pair), bf16),
            pltpu.VMEM((global_count, pair), jnp.float32),
            pltpu.VMEM((shards, 8, pair), jnp.int32),
            pltpu.SMEM((shards, 8, pair), jnp.int32),
            pltpu.SemaphoreType.DMA,
        ],
        compiler_params=params,
    )(place.reshape(1, -1), place.reshape(-1, 1), whole.reshape(shards * stride, 2 * pair))
    returned = lax.all_to_all(result, "seq", split_axis=0, concat_axis=0, tiled=True)
    return pl.pallas_call(unpack_kernel, out_shape=(narrow,) * 4, compiler_params=params)(returned)


def body(queries, *others):
    shards = lax.axis_size("seq")
    tokens, width = queries.shape
    if width // HEAD_DIM <= shards and shards * tokens <= WHOLE_ROWS:
        return whole_body(queries, *others)
    return sparse_body(queries, *others)


def solution(mesh):
    in_specs = (
        P(("groups", "seq"), "head"),
        P(("groups", "seq"), "head"),
        P(("groups", "seq"), "head"),
        P(("groups", "seq"), "head"),
        P(("groups", "seq"), "head", None),
        P("groups"),
    )
    out_specs = (
        P(("groups", "seq"), "head"),
        P(("groups", "seq"), "head"),
        P(("groups", "seq"), "head"),
        P(("groups", "seq"), "head"),
    )
    return jax.shard_map(body, mesh=mesh, in_specs=in_specs, out_specs=out_specs, check_vma=False)
```

```python
import math

import jax
import jax.numpy as jnp
from jax import lax
from jax.experimental import pallas as pl
from jax.experimental.pallas import tpu as pltpu
from jax.sharding import PartitionSpec as P

HEAD_DIM = 64
BLOCK = 64
RAND = 3


MASKED = -1e30


def with_halo(array, sides, width):
    for axis, dim in sides:
        size, length = (lax.axis_size(axis), array.shape[dim])
        up = [(i, (i + 1) % size) for i in range(size - 1)]
        down = [(j, i) for i, j in up]
        last = lax.slice_in_dim(array, length - width, length, axis=dim)
        initial = lax.slice_in_dim(array, 0, width, axis=dim)
        before = lax.ppermute(last, axis, up)
        after = lax.ppermute(initial, axis, down)
        array = jnp.concatenate([before, array, after], axis=dim)
    return array


def attend_head(
    query, key_rows, value_rows, visible, global_keys, global_values, grad_out, score_scale
):
    local_score = (
        jnp.einsum("nqe,nke->nqk", query, key_rows, preferred_element_type=jnp.float32)
        * score_scale
    )
    local_score = jnp.where(visible, local_score, MASKED)
    global_score = (
        jnp.einsum("nqe,ke->nqk", query, global_keys, preferred_element_type=jnp.float32)
        * score_scale
    )
    highest = jnp.maximum(
        jnp.max(local_score, axis=-1, keepdims=True), jnp.max(global_score, axis=-1, keepdims=True)
    )
    local_exp = jnp.exp(local_score - highest)
    global_exp = jnp.exp(global_score - highest)
    totals = jnp.sum(local_exp, axis=-1, keepdims=True) + jnp.sum(
        global_exp, axis=-1, keepdims=True
    )
    local_weight = (local_exp / totals).astype(jnp.bfloat16)
    global_weight = (global_exp / totals).astype(jnp.bfloat16)
    outputs = (
        jnp.einsum("nqk,nke->nqe", local_weight, value_rows, preferred_element_type=jnp.float32)
        + jnp.einsum(
            "nqk,ke->nqe", global_weight, global_values, preferred_element_type=jnp.float32
        )
    ).astype(jnp.bfloat16)
    local_dp = jnp.einsum("nqe,nke->nqk", grad_out, value_rows, preferred_element_type=jnp.float32)
    global_dp = jnp.einsum(
        "nqe,ke->nqk", grad_out, global_values, preferred_element_type=jnp.float32
    )
    local_wf = local_weight.astype(jnp.float32)
    global_wf = global_weight.astype(jnp.float32)
    delta_sum = jnp.sum(local_wf * local_dp, axis=-1, keepdims=True) + jnp.sum(
        global_wf * global_dp, axis=-1, keepdims=True
    )
    local_ds = (local_wf * (local_dp - delta_sum) * score_scale).astype(jnp.bfloat16)
    global_ds = (global_wf * (global_dp - delta_sum) * score_scale).astype(jnp.bfloat16)
    grad_query = (
        jnp.einsum("nqk,nke->nqe", local_ds, key_rows, preferred_element_type=jnp.float32)
        + jnp.einsum("nqk,ke->nqe", global_ds, global_keys, preferred_element_type=jnp.float32)
    ).astype(jnp.bfloat16)
    local_dk = jnp.einsum("nqk,nqe->nke", local_ds, query, preferred_element_type=jnp.float32)
    local_dv = jnp.einsum(
        "nqk,nqe->nke", local_weight, grad_out, preferred_element_type=jnp.float32
    )
    global_dk = jnp.einsum("nqk,nqe->ke", global_ds, query, preferred_element_type=jnp.float32)
    global_dv = jnp.einsum(
        "nqk,nqe->ke", global_weight, grad_out, preferred_element_type=jnp.float32
    )
    return (outputs, grad_query, local_dk, local_dv, global_dk, global_dv, local_ds, local_weight)


def sparse_body(queries, key_input, value_input, grad_output, rand_blocks, global_pos):
    tokens = queries.shape[0]
    blocks = tokens // BLOCK
    head_count = queries.shape[1] // HEAD_DIM
    pair_width = 2 * HEAD_DIM
    shards = lax.axis_size("seq")
    own_index = lax.axis_index("seq")
    first_row = own_index * tokens
    score_scale = 1.0 / math.sqrt(HEAD_DIM)
    packed_kv = jnp.concatenate(
        (
            key_input.reshape(tokens, head_count, HEAD_DIM),
            value_input.reshape(tokens, head_count, HEAD_DIM),
        ),
        axis=2,
    )
    padded = with_halo(packed_kv, (("seq", 0),), BLOCK)
    window_kv = jnp.concatenate(
        [
            padded[offset * BLOCK : offset * BLOCK + tokens].reshape(
                blocks, BLOCK, head_count, pair_width
            )
            for offset in range(3)
        ],
        axis=1,
    ).transpose(2, 0, 1, 3)
    request_block = rand_blocks.reshape(-1)
    requests = request_block.shape[0]
    request_ids = jnp.arange(requests, dtype=jnp.int32)
    request_head = request_ids // RAND % head_count
    owner_shard = request_block // blocks
    capacity = max(2, (requests + shards - 1) // shards)
    slots_all = shards * capacity
    earlier = (owner_shard[:, None] == owner_shard[None, :]) & (
        request_ids[None, :] < request_ids[:, None]
    )
    slot_rank = jnp.sum(earlier.astype(jnp.int32), axis=1)
    request_slot = owner_shard * capacity + slot_rank
    slot_match = request_slot[None, :] == jnp.arange(slots_all, dtype=jnp.int32)[:, None]
    slot_used = jnp.any(slot_match, axis=1)
    slot_source = jnp.sum(jnp.where(slot_match, request_ids[None, :], 0), axis=1)
    request_code = request_block % blocks * head_count + request_head
    wanted = jnp.where(slot_used, jnp.take(request_code, slot_source), -1).reshape(shards, capacity)
    block_table = (
        packed_kv.reshape(blocks, BLOCK, head_count, pair_width)
        .transpose(0, 2, 1, 3)
        .reshape(blocks * head_count, BLOCK, pair_width)
    )
    asked_codes = lax.all_to_all(wanted, "seq", split_axis=0, concat_axis=0, tiled=True)
    picked = jnp.take(block_table, jnp.maximum(asked_codes, 0), axis=0)
    fetched, asked_codes = (
        lax.all_to_all(picked, "seq", split_axis=0, concat_axis=0, tiled=True),
        asked_codes,
    )
    random_kv = jnp.take(fetched.reshape(slots_all, BLOCK, pair_width), request_slot, axis=0)
    random_kv = random_kv.reshape(blocks, head_count, RAND * BLOCK, pair_width).transpose(
        1, 0, 2, 3
    )
    local_kv = jnp.concatenate((window_kv, random_kv), axis=2)
    block_ids = own_index * blocks + jnp.arange(blocks, dtype=jnp.int32)
    neighbour = block_ids[:, None] + jnp.arange(3, dtype=jnp.int32)[None, :] - 1
    inside = (neighbour >= 0) & (neighbour < blocks * shards)
    visible = jnp.concatenate(
        (jnp.repeat(inside, BLOCK, axis=1), jnp.ones((blocks, RAND * BLOCK), jnp.bool_)), axis=1
    )[:, None, :]
    global_count = global_pos.shape[0]
    global_ids = jnp.arange(global_count, dtype=jnp.int32)
    row_ids = jnp.arange(tokens, dtype=jnp.int32)
    flat_kv = packed_kv.reshape(tokens, head_count * pair_width)
    row_match = global_pos[:, None] == first_row + row_ids[None, :]
    partial_rows = jnp.dot(
        row_match.astype(jnp.bfloat16), flat_kv, preferred_element_type=jnp.float32
    )
    global_kv = lax.psum(partial_rows, "seq").astype(jnp.bfloat16)
    global_kv = global_kv.reshape(global_count, head_count, pair_width).transpose(1, 0, 2)

    def heads_first(array):
        return array.reshape(blocks, BLOCK, head_count, HEAD_DIM).transpose(2, 0, 1, 3)

    query_heads = heads_first(queries)
    grad_heads = heads_first(grad_output)

    def one_head(operands):
        query, local_pair, global_pair, grad_out = operands
        return attend_head(
            query,
            local_pair[..., :HEAD_DIM],
            local_pair[..., HEAD_DIM:],
            visible,
            global_pair[:, :HEAD_DIM],
            global_pair[:, HEAD_DIM:],
            grad_out,
            score_scale,
        )

    outputs, grad_query, local_dk, local_dv, global_dk, global_dv, local_ds, local_weight = lax.map(
        one_head, (query_heads, local_kv, global_kv, grad_heads)
    )

    def rows_last(array):
        return array.transpose(1, 2, 0, 3).reshape(tokens, head_count * HEAD_DIM)

    local_grad = jnp.concatenate((local_dk, local_dv), axis=3)
    window_grad = local_grad[:, :, : 3 * BLOCK].transpose(1, 2, 0, 3)
    spread = sum(
        (
            jnp.pad(
                window_grad[:, offset * BLOCK : (offset + 1) * BLOCK].reshape(
                    tokens, head_count, pair_width
                ),
                ((offset * BLOCK, (2 - offset) * BLOCK), (0, 0), (0, 0)),
            )
            for offset in range(3)
        )
    )
    rim_pair = jnp.concatenate((spread[:BLOCK], spread[-BLOCK:]), axis=0)
    rim_in = with_halo(rim_pair.astype(jnp.bfloat16), (("seq", 0),), BLOCK).astype(rim_pair.dtype)
    window_total = (
        spread[BLOCK:-BLOCK]
        + jnp.pad(rim_in[:BLOCK], ((0, tokens - BLOCK), (0, 0), (0, 0)))
        + jnp.pad(rim_in[-BLOCK:], ((tokens - BLOCK, 0), (0, 0), (0, 0)))
    )
    random_grad = local_grad[:, :, 3 * BLOCK :].reshape(head_count, blocks, RAND, BLOCK, pair_width)
    random_grad = (
        random_grad.transpose(1, 0, 2, 3, 4)
        .reshape(requests, BLOCK, pair_width)
        .astype(jnp.bfloat16)
    )
    outgoing = jnp.where(slot_used[:, None, None], jnp.take(random_grad, slot_source, axis=0), 0)
    returned = lax.all_to_all(
        outgoing.reshape(shards, capacity, BLOCK, pair_width),
        "seq",
        split_axis=0,
        concat_axis=0,
        tiled=True,
    )
    target = (
        asked_codes.reshape(-1)[None, :]
        == jnp.arange(blocks * head_count, dtype=jnp.int32)[:, None]
    ).astype(jnp.bfloat16)
    random_total = jnp.dot(
        target, returned.reshape(slots_all, BLOCK * pair_width), preferred_element_type=jnp.float32
    )
    random_total = (
        random_total.reshape(blocks, head_count, BLOCK, pair_width)
        .transpose(0, 2, 1, 3)
        .reshape(tokens, head_count, pair_width)
    )
    global_grad = (
        jnp.concatenate((global_dk, global_dv), axis=2)
        .transpose(1, 0, 2)
        .reshape(global_count, head_count * pair_width)
    )
    global_total = lax.psum(global_grad, "seq")
    row_source = jnp.sum(jnp.where(row_match, global_ids[:, None], 0), axis=0)
    row_used = jnp.any(row_match, axis=0)
    global_rows = jnp.where(row_used[:, None], jnp.take(global_total, row_source, axis=0), 0.0)
    grand_total = window_total + random_total + global_rows.reshape(tokens, head_count, pair_width)
    key_rows_out = (
        grand_total[..., :HEAD_DIM].reshape(tokens, head_count * HEAD_DIM).astype(jnp.bfloat16)
    )
    value_rows_out = (
        grand_total[..., HEAD_DIM:].reshape(tokens, head_count * HEAD_DIM).astype(jnp.bfloat16)
    )
    return (rows_last(outputs), rows_last(grad_query), key_rows_out, value_rows_out)


WHOLE_ROWS = 4096
GROUP = 4
VMEM_BYTES = 32 * 1024 * 1024


def dot(left, right, left_dim, right_dim):
    return lax.dot_general(
        left,
        right,
        (((left_dim,), (right_dim,)), ((), ())),
        preferred_element_type=jnp.float32,
    )


def listed_rows(tokens):
    return -(-(tokens // BLOCK * RAND) // 16) * 16


def pack_kernel(rand_hbm, key_hbm, value_hbm, query_hbm, grad_hbm, packed_ref, *scratch):
    *targets, listed, sems = scratch
    _, key_ref, value_ref, query_ref, grad_ref = targets
    tokens, width = key_ref.shape
    heads = width // HEAD_DIM
    copies = [
        pltpu.make_async_copy(source, target, sems.at[i])
        for i, (source, target) in enumerate(
            zip((rand_hbm, key_hbm, value_hbm, query_hbm, grad_hbm), targets)
        )
    ]
    for copy in copies:
        copy.start()
    listed[...] = jnp.zeros_like(listed)
    for slot in range(heads, packed_ref.shape[0]):
        packed_ref[slot] = jnp.zeros(packed_ref.shape[1:], jnp.bfloat16)
    for copy in copies:
        copy.wait()
    for block in range(tokens // BLOCK):
        listed[block * RAND : (block + 1) * RAND, :heads] = targets[0][block]
    entries = listed[...].astype(jnp.float32).astype(jnp.bfloat16)
    for head in range(heads):
        cols = slice(head * HEAD_DIM, (head + 1) * HEAD_DIM)
        packed_ref[head, :tokens, : 2 * HEAD_DIM] = jnp.concatenate(
            (key_ref[:, cols], value_ref[:, cols]), axis=1
        )
        packed_ref[head, :tokens, 2 * HEAD_DIM :] = jnp.concatenate(
            (query_ref[:, cols], grad_ref[:, cols]), axis=1
        )
        packed_ref[head, tokens:, : 2 * HEAD_DIM] = entries
        packed_ref[head, tokens:, 2 * HEAD_DIM :] = jnp.zeros_like(entries)


def unpack_kernel(packed_ref, attended_ref, query_ref, key_ref, value_ref):
    heads = key_ref.shape[1] // HEAD_DIM
    for head in range(heads):
        cols = slice(head * HEAD_DIM, (head + 1) * HEAD_DIM)
        for i, ref in enumerate((query_ref, attended_ref, key_ref, value_ref)):
            ref[:, cols] = packed_ref[head, :, i * HEAD_DIM : (i + 1) * HEAD_DIM]


def attend_kernel(
    pos_row_ref, pos_col_ref, x_ref, out_ref, acc, global_kv, global_acc, listed, starts, sem
):
    shards, tokens, _ = out_ref.shape
    stride = x_ref.shape[0] // shards
    blocks = tokens // BLOCK
    global_count = pos_row_ref.shape[1]
    own = lax.axis_index("seq")
    kv_cols = slice(0, 2 * HEAD_DIM)
    rest_cols = slice(2 * HEAD_DIM, 4 * HEAD_DIM)

    for shard in range(shards):
        row = x_ref[shard * stride + tokens : (shard + 1) * stride, kv_cols].astype(jnp.float32)
        passed = jnp.floor((row + 0.5) * (1.0 / blocks))
        first = row * BLOCK + passed * (stride - tokens)
        listed[shard] = first.astype(jnp.int32)
    copy = pltpu.make_async_copy(listed, starts, sem)
    copy.start()
    acc[...] = jnp.zeros_like(acc)
    global_acc[...] = jnp.zeros_like(global_acc)
    place = lax.broadcasted_iota(jnp.int32, (global_count, shards * stride), 1)
    pick = (place == pos_col_ref[...]).astype(jnp.bfloat16)
    global_kv[...] = dot(pick, x_ref[:, kv_cols], 1, 0).astype(jnp.bfloat16)
    copy.wait()
    lane = lax.broadcasted_iota(jnp.int32, (BLOCK, 6 * BLOCK), 1)
    half = lax.broadcasted_iota(jnp.int32, (BLOCK, 2 * HEAD_DIM), 1) < HEAD_DIM
    query_mask = jnp.where(half, 1.0 / math.sqrt(HEAD_DIM), 0.0).astype(jnp.bfloat16)
    grad_mask = jnp.where(half, 0.0, 1.0).astype(jnp.bfloat16)

    def at(start):
        return pl.ds(pl.multiple_of(start, 16), BLOCK)

    def products(shard):
        base = shard * stride
        before = jnp.maximum(shard - 1, 0) * stride + (blocks - 1) * BLOCK
        after = jnp.minimum(shard + 1, shards - 1) * stride
        rows = []
        for block in range(blocks):
            rest = x_ref[at(base + block * BLOCK), rest_cols]
            rows += [rest * query_mask, rest * grad_mask]
        rows = jnp.concatenate(rows, axis=0)
        all_places, local_kvs, local_dots = [], [], []
        for block in range(blocks):
            places = [
                base + (block - 1) * BLOCK if block else before,
                base + block * BLOCK,
                base + (block + 1) * BLOCK if block < blocks - 1 else after,
            ] + [starts[shard, block * RAND + r, own] for r in range(RAND)]
            all_places.append([at(p) for p in places])
            local_kvs.append(jnp.concatenate([x_ref[p, kv_cols] for p in all_places[-1]], axis=0))
            both = rows[2 * block * BLOCK : 2 * (block + 1) * BLOCK]
            local_dots.append(dot(both, local_kvs[-1], 1, 1))
        return rows, all_places, local_kvs, local_dots, dot(rows, global_kv[...], 1, 1)

    def weigh(shard, block, local_dots, global_dots):
        score, dp = local_dots[:BLOCK], local_dots[BLOCK:]
        if block == 0:
            score = jnp.where((lane < BLOCK) & (shard == 0), MASKED, score)
        if block == blocks - 1:
            outside = (lane >= 2 * BLOCK) & (lane < 3 * BLOCK)
            score = jnp.where(outside & (shard == shards - 1), MASKED, score)
        global_score, global_dp = global_dots[:BLOCK], global_dots[BLOCK:]
        highest = jnp.maximum(
            jnp.max(score, axis=1, keepdims=True),
            jnp.max(global_score, axis=1, keepdims=True),
        )
        local_exp = jnp.exp(score - highest)
        global_exp = jnp.exp(global_score - highest)
        inverse = 1.0 / (
            jnp.sum(local_exp, axis=1, keepdims=True)
            + jnp.sum(global_exp, axis=1, keepdims=True)
        )
        local_weight = (local_exp * inverse).astype(jnp.bfloat16)
        global_weight = (global_exp * inverse).astype(jnp.bfloat16)
        local_wf = local_weight.astype(jnp.float32)
        global_wf = global_weight.astype(jnp.float32)
        delta = jnp.sum(local_wf * dp, axis=1, keepdims=True) + jnp.sum(
            global_wf * global_dp, axis=1, keepdims=True
        )
        local_ds = (local_wf * (dp - delta)).astype(jnp.bfloat16)
        global_ds = (global_wf * (global_dp - delta)).astype(jnp.bfloat16)
        return (
            jnp.concatenate((local_ds, local_weight), axis=0),
            jnp.concatenate((global_ds, global_weight), axis=0),
        )

    def shard_group(group, carry):
        members = [group * GROUP + i for i in range(GROUP)]
        made = [products(shard) for shard in members]
        sides = [
            [
                weigh(
                    shard,
                    block,
                    local_dots[block],
                    global_dots[2 * block * BLOCK : 2 * (block + 1) * BLOCK],
                )
                for block in range(blocks)
            ]
            for shard, (_, _, _, local_dots, global_dots) in zip(members, made)
        ]
        gkv = global_kv[...]
        for shard, side, (rows, all_places, local_kvs, _, _) in zip(members, sides, made):
            global_side = jnp.concatenate([pair[1] for pair in side], axis=0)
            global_result = dot(global_side, gkv, 1, 0)
            results, grads = [], []
            for block in range(blocks):
                span = slice(2 * block * BLOCK, 2 * (block + 1) * BLOCK)
                results.append(dot(side[block][0], local_kvs[block], 1, 0) + global_result[span])
                grads.append(dot(side[block][0], rows[span], 0, 0))
            global_acc[...] += dot(global_side, rows, 0, 0)
            for block in range(blocks):
                out_ref[shard, block * BLOCK : (block + 1) * BLOCK, kv_cols] = jnp.where(
                    half,
                    results[block][:BLOCK] * (1.0 / math.sqrt(HEAD_DIM)),
                    results[block][BLOCK:],
                ).astype(jnp.bfloat16)
                for i, spot in enumerate(all_places[block]):
                    acc[spot] += grads[block][i * BLOCK : (i + 1) * BLOCK]
        return carry

    lax.fori_loop(0, shards // GROUP, shard_group, 0)
    global_grad = global_acc[...].astype(jnp.bfloat16)
    for shard in range(shards):
        place = shard * stride + lax.broadcasted_iota(jnp.int32, (tokens, global_count), 0)
        spread = (place == pos_row_ref[...]).astype(jnp.bfloat16)
        out_ref[shard, :, rest_cols] = (
            acc[shard * stride : shard * stride + tokens] + dot(spread, global_grad, 1, 0)
        ).astype(jnp.bfloat16)


def attend(whole, place):
    shards, stride, _ = whole.shape
    tokens = stride - listed_rows(stride - stride % BLOCK)
    extra = stride - tokens
    pair = 2 * HEAD_DIM
    global_count = place.shape[0]
    return pl.pallas_call(
        attend_kernel,
        out_shape=jax.ShapeDtypeStruct((shards, tokens, 2 * pair), jnp.bfloat16),
        scratch_shapes=[
            pltpu.VMEM((shards * stride, pair), jnp.float32),
            pltpu.VMEM((global_count, pair), jnp.bfloat16),
            pltpu.VMEM((global_count, pair), jnp.float32),
            pltpu.VMEM((shards, extra, pair), jnp.int32),
            pltpu.SMEM((shards, extra, pair), jnp.int32),
            pltpu.SemaphoreType.DMA,
        ],
        compiler_params=pltpu.CompilerParams(vmem_limit_bytes=VMEM_BYTES),
    )(place.reshape(1, -1), place.reshape(-1, 1), whole.reshape(shards * stride, 2 * pair))


def whole_body(queries, key_input, value_input, grad_output, rand_blocks, global_pos):
    tokens, width = queries.shape
    shards = lax.axis_size("seq")
    extra = listed_rows(tokens)
    stride = tokens + extra
    narrow = jax.ShapeDtypeStruct((tokens, width), jnp.bfloat16)
    rand_lists = rand_blocks.transpose(0, 2, 1)
    packed = pl.pallas_call(
        pack_kernel,
        out_shape=jax.ShapeDtypeStruct((shards, stride, 4 * HEAD_DIM), jnp.bfloat16),
        in_specs=[pl.BlockSpec(memory_space=pl.ANY)] * 5,
        scratch_shapes=[pltpu.VMEM(rand_lists.shape, jnp.int32)]
        + [pltpu.VMEM((tokens, width), jnp.bfloat16)] * 4
        + [
            pltpu.VMEM((extra, 2 * HEAD_DIM), jnp.int32),
            pltpu.SemaphoreType.DMA((5,)),
        ],
    )(rand_lists, key_input, value_input, queries, grad_output)
    whole = lax.all_to_all(packed, "seq", split_axis=0, concat_axis=0, tiled=True)
    result = attend(whole, global_pos + global_pos // tokens * extra)
    returned = lax.all_to_all(result, "seq", split_axis=0, concat_axis=0, tiled=True)
    return pl.pallas_call(
        unpack_kernel,
        out_shape=(narrow,) * 4,
        compiler_params=pltpu.CompilerParams(vmem_limit_bytes=VMEM_BYTES),
    )(returned)


def body(queries, *others):
    shards = lax.axis_size("seq")
    tokens, width = queries.shape
    if width // HEAD_DIM <= shards and shards * tokens <= WHOLE_ROWS:
        return whole_body(queries, *others)
    return sparse_body(queries, *others)


def solution(mesh):
    in_specs = (
        P(("groups", "seq"), "head"),
        P(("groups", "seq"), "head"),
        P(("groups", "seq"), "head"),
        P(("groups", "seq"), "head"),
        P(("groups", "seq"), "head", None),
        P("groups"),
    )
    out_specs = (
        P(("groups", "seq"), "head"),
        P(("groups", "seq"), "head"),
        P(("groups", "seq"), "head"),
        P(("groups", "seq"), "head"),
    )
    return jax.shard_map(body, mesh=mesh, in_specs=in_specs, out_specs=out_specs, check_vma=False)
```

```python
import math

import jax
import jax.numpy as jnp
from jax import lax
from jax.experimental import pallas as pl
from jax.experimental.pallas import tpu as pltpu
from jax.sharding import PartitionSpec as P

HEAD_DIM = 64
BLOCK = 64
RAND = 3


MASKED = -1e30


def with_halo(array, sides, width):
    for axis, dim in sides:
        size, length = (lax.axis_size(axis), array.shape[dim])
        up = [(i, (i + 1) % size) for i in range(size - 1)]
        down = [(j, i) for i, j in up]
        last = lax.slice_in_dim(array, length - width, length, axis=dim)
        initial = lax.slice_in_dim(array, 0, width, axis=dim)
        before = lax.ppermute(last, axis, up)
        after = lax.ppermute(initial, axis, down)
        array = jnp.concatenate([before, array, after], axis=dim)
    return array


def attend_head(
    query, key_rows, value_rows, visible, global_keys, global_values, grad_out, score_scale
):
    local_score = (
        jnp.einsum("nqe,nke->nqk", query, key_rows, preferred_element_type=jnp.float32)
        * score_scale
    )
    local_score = jnp.where(visible, local_score, MASKED)
    global_score = (
        jnp.einsum("nqe,ke->nqk", query, global_keys, preferred_element_type=jnp.float32)
        * score_scale
    )
    highest = jnp.maximum(
        jnp.max(local_score, axis=-1, keepdims=True), jnp.max(global_score, axis=-1, keepdims=True)
    )
    local_exp = jnp.exp(local_score - highest)
    global_exp = jnp.exp(global_score - highest)
    totals = jnp.sum(local_exp, axis=-1, keepdims=True) + jnp.sum(
        global_exp, axis=-1, keepdims=True
    )
    local_weight = (local_exp / totals).astype(jnp.bfloat16)
    global_weight = (global_exp / totals).astype(jnp.bfloat16)
    outputs = (
        jnp.einsum("nqk,nke->nqe", local_weight, value_rows, preferred_element_type=jnp.float32)
        + jnp.einsum(
            "nqk,ke->nqe", global_weight, global_values, preferred_element_type=jnp.float32
        )
    ).astype(jnp.bfloat16)
    local_dp = jnp.einsum("nqe,nke->nqk", grad_out, value_rows, preferred_element_type=jnp.float32)
    global_dp = jnp.einsum(
        "nqe,ke->nqk", grad_out, global_values, preferred_element_type=jnp.float32
    )
    local_wf = local_weight.astype(jnp.float32)
    global_wf = global_weight.astype(jnp.float32)
    delta_sum = jnp.sum(local_wf * local_dp, axis=-1, keepdims=True) + jnp.sum(
        global_wf * global_dp, axis=-1, keepdims=True
    )
    local_ds = (local_wf * (local_dp - delta_sum) * score_scale).astype(jnp.bfloat16)
    global_ds = (global_wf * (global_dp - delta_sum) * score_scale).astype(jnp.bfloat16)
    grad_query = (
        jnp.einsum("nqk,nke->nqe", local_ds, key_rows, preferred_element_type=jnp.float32)
        + jnp.einsum("nqk,ke->nqe", global_ds, global_keys, preferred_element_type=jnp.float32)
    ).astype(jnp.bfloat16)
    local_dk = jnp.einsum("nqk,nqe->nke", local_ds, query, preferred_element_type=jnp.float32)
    local_dv = jnp.einsum(
        "nqk,nqe->nke", local_weight, grad_out, preferred_element_type=jnp.float32
    )
    global_dk = jnp.einsum("nqk,nqe->ke", global_ds, query, preferred_element_type=jnp.float32)
    global_dv = jnp.einsum(
        "nqk,nqe->ke", global_weight, grad_out, preferred_element_type=jnp.float32
    )
    return (outputs, grad_query, local_dk, local_dv, global_dk, global_dv, local_ds, local_weight)


def sparse_body(queries, key_input, value_input, grad_output, rand_blocks, global_pos):
    tokens = queries.shape[0]
    blocks = tokens // BLOCK
    head_count = queries.shape[1] // HEAD_DIM
    pair_width = 2 * HEAD_DIM
    shards = lax.axis_size("seq")
    own_index = lax.axis_index("seq")
    first_row = own_index * tokens
    score_scale = 1.0 / math.sqrt(HEAD_DIM)
    packed_kv = jnp.concatenate(
        (
            key_input.reshape(tokens, head_count, HEAD_DIM),
            value_input.reshape(tokens, head_count, HEAD_DIM),
        ),
        axis=2,
    )
    padded = with_halo(packed_kv, (("seq", 0),), BLOCK)
    window_kv = jnp.concatenate(
        [
            padded[offset * BLOCK : offset * BLOCK + tokens].reshape(
                blocks, BLOCK, head_count, pair_width
            )
            for offset in range(3)
        ],
        axis=1,
    ).transpose(2, 0, 1, 3)
    request_block = rand_blocks.reshape(-1)
    requests = request_block.shape[0]
    request_ids = jnp.arange(requests, dtype=jnp.int32)
    request_head = request_ids // RAND % head_count
    owner_shard = request_block // blocks
    capacity = max(2, (requests + shards - 1) // shards)
    slots_all = shards * capacity
    earlier = (owner_shard[:, None] == owner_shard[None, :]) & (
        request_ids[None, :] < request_ids[:, None]
    )
    slot_rank = jnp.sum(earlier.astype(jnp.int32), axis=1)
    request_slot = owner_shard * capacity + slot_rank
    slot_match = request_slot[None, :] == jnp.arange(slots_all, dtype=jnp.int32)[:, None]
    slot_used = jnp.any(slot_match, axis=1)
    slot_source = jnp.sum(jnp.where(slot_match, request_ids[None, :], 0), axis=1)
    request_code = request_block % blocks * head_count + request_head
    wanted = jnp.where(slot_used, jnp.take(request_code, slot_source), -1).reshape(shards, capacity)
    block_table = (
        packed_kv.reshape(blocks, BLOCK, head_count, pair_width)
        .transpose(0, 2, 1, 3)
        .reshape(blocks * head_count, BLOCK, pair_width)
    )
    asked_codes = lax.all_to_all(wanted, "seq", split_axis=0, concat_axis=0, tiled=True)
    picked = jnp.take(block_table, jnp.maximum(asked_codes, 0), axis=0)
    fetched, asked_codes = (
        lax.all_to_all(picked, "seq", split_axis=0, concat_axis=0, tiled=True),
        asked_codes,
    )
    random_kv = jnp.take(fetched.reshape(slots_all, BLOCK, pair_width), request_slot, axis=0)
    random_kv = random_kv.reshape(blocks, head_count, RAND * BLOCK, pair_width).transpose(
        1, 0, 2, 3
    )
    local_kv = jnp.concatenate((window_kv, random_kv), axis=2)
    block_ids = own_index * blocks + jnp.arange(blocks, dtype=jnp.int32)
    neighbour = block_ids[:, None] + jnp.arange(3, dtype=jnp.int32)[None, :] - 1
    inside = (neighbour >= 0) & (neighbour < blocks * shards)
    visible = jnp.concatenate(
        (jnp.repeat(inside, BLOCK, axis=1), jnp.ones((blocks, RAND * BLOCK), jnp.bool_)), axis=1
    )[:, None, :]
    global_count = global_pos.shape[0]
    global_ids = jnp.arange(global_count, dtype=jnp.int32)
    row_ids = jnp.arange(tokens, dtype=jnp.int32)
    flat_kv = packed_kv.reshape(tokens, head_count * pair_width)
    row_match = global_pos[:, None] == first_row + row_ids[None, :]
    partial_rows = jnp.dot(
        row_match.astype(jnp.bfloat16), flat_kv, preferred_element_type=jnp.float32
    )
    global_kv = lax.psum(partial_rows, "seq").astype(jnp.bfloat16)
    global_kv = global_kv.reshape(global_count, head_count, pair_width).transpose(1, 0, 2)

    def heads_first(array):
        return array.reshape(blocks, BLOCK, head_count, HEAD_DIM).transpose(2, 0, 1, 3)

    query_heads = heads_first(queries)
    grad_heads = heads_first(grad_output)

    def one_head(operands):
        query, local_pair, global_pair, grad_out = operands
        return attend_head(
            query,
            local_pair[..., :HEAD_DIM],
            local_pair[..., HEAD_DIM:],
            visible,
            global_pair[:, :HEAD_DIM],
            global_pair[:, HEAD_DIM:],
            grad_out,
            score_scale,
        )

    outputs, grad_query, local_dk, local_dv, global_dk, global_dv, local_ds, local_weight = lax.map(
        one_head, (query_heads, local_kv, global_kv, grad_heads)
    )

    def rows_last(array):
        return array.transpose(1, 2, 0, 3).reshape(tokens, head_count * HEAD_DIM)

    local_grad = jnp.concatenate((local_dk, local_dv), axis=3)
    window_grad = local_grad[:, :, : 3 * BLOCK].transpose(1, 2, 0, 3)
    spread = sum(
        (
            jnp.pad(
                window_grad[:, offset * BLOCK : (offset + 1) * BLOCK].reshape(
                    tokens, head_count, pair_width
                ),
                ((offset * BLOCK, (2 - offset) * BLOCK), (0, 0), (0, 0)),
            )
            for offset in range(3)
        )
    )
    rim_pair = jnp.concatenate((spread[:BLOCK], spread[-BLOCK:]), axis=0)
    rim_in = with_halo(rim_pair.astype(jnp.bfloat16), (("seq", 0),), BLOCK).astype(rim_pair.dtype)
    window_total = (
        spread[BLOCK:-BLOCK]
        + jnp.pad(rim_in[:BLOCK], ((0, tokens - BLOCK), (0, 0), (0, 0)))
        + jnp.pad(rim_in[-BLOCK:], ((tokens - BLOCK, 0), (0, 0), (0, 0)))
    )
    random_grad = local_grad[:, :, 3 * BLOCK :].reshape(head_count, blocks, RAND, BLOCK, pair_width)
    random_grad = (
        random_grad.transpose(1, 0, 2, 3, 4)
        .reshape(requests, BLOCK, pair_width)
        .astype(jnp.bfloat16)
    )
    outgoing = jnp.where(slot_used[:, None, None], jnp.take(random_grad, slot_source, axis=0), 0)
    returned = lax.all_to_all(
        outgoing.reshape(shards, capacity, BLOCK, pair_width),
        "seq",
        split_axis=0,
        concat_axis=0,
        tiled=True,
    )
    target = (
        asked_codes.reshape(-1)[None, :]
        == jnp.arange(blocks * head_count, dtype=jnp.int32)[:, None]
    ).astype(jnp.bfloat16)
    random_total = jnp.dot(
        target, returned.reshape(slots_all, BLOCK * pair_width), preferred_element_type=jnp.float32
    )
    random_total = (
        random_total.reshape(blocks, head_count, BLOCK, pair_width)
        .transpose(0, 2, 1, 3)
        .reshape(tokens, head_count, pair_width)
    )
    global_grad = (
        jnp.concatenate((global_dk, global_dv), axis=2)
        .transpose(1, 0, 2)
        .reshape(global_count, head_count * pair_width)
    )
    global_total = lax.psum(global_grad, "seq")
    row_source = jnp.sum(jnp.where(row_match, global_ids[:, None], 0), axis=0)
    row_used = jnp.any(row_match, axis=0)
    global_rows = jnp.where(row_used[:, None], jnp.take(global_total, row_source, axis=0), 0.0)
    grand_total = window_total + random_total + global_rows.reshape(tokens, head_count, pair_width)
    key_rows_out = (
        grand_total[..., :HEAD_DIM].reshape(tokens, head_count * HEAD_DIM).astype(jnp.bfloat16)
    )
    value_rows_out = (
        grand_total[..., HEAD_DIM:].reshape(tokens, head_count * HEAD_DIM).astype(jnp.bfloat16)
    )
    return (rows_last(outputs), rows_last(grad_query), key_rows_out, value_rows_out)


WHOLE_ROWS = 4096
GROUP = 4
VMEM_BYTES = 32 * 1024 * 1024


def dot(left, right, left_dim, right_dim):
    return lax.dot_general(
        left,
        right,
        (((left_dim,), (right_dim,)), ((), ())),
        preferred_element_type=jnp.float32,
    )


def listed_rows(tokens):
    return -(-(tokens // BLOCK * RAND) // 16) * 16


def pack_kernel(rand_hbm, key_hbm, value_hbm, query_hbm, grad_hbm, packed_hbm, *scratch):
    *targets, listed, packed, sems, out_sems = scratch
    rand_ref, key_ref, value_ref, query_ref, grad_ref = targets
    tokens, width = key_ref.shape
    heads = width // HEAD_DIM
    slots = packed.shape[0]
    copies = [
        pltpu.make_async_copy(source, target, sems.at[i])
        for i, (source, target) in enumerate(
            zip((rand_hbm, key_hbm, value_hbm, query_hbm, grad_hbm), targets)
        )
    ]
    sends = [
        pltpu.make_async_copy(packed.at[slot], packed_hbm.at[slot], out_sems.at[slot])
        for slot in range(slots)
    ]
    for copy in copies:
        copy.start()
    listed[...] = jnp.zeros_like(listed)
    for slot in range(heads, slots):
        packed[slot] = jnp.zeros(packed.shape[1:], jnp.bfloat16)
        sends[slot].start()
    for copy in copies:
        copy.wait()
    for block in range(tokens // BLOCK):
        listed[block * RAND : (block + 1) * RAND, :heads] = rand_ref[block]
    entries = listed[...].astype(jnp.float32).astype(jnp.bfloat16)
    for head in range(heads):
        cols = slice(head * HEAD_DIM, (head + 1) * HEAD_DIM)
        packed[head, :tokens] = jnp.concatenate((key_ref[:, cols], value_ref[:, cols]), axis=1)
        packed[head, tokens : 2 * tokens] = jnp.concatenate(
            (query_ref[:, cols], grad_ref[:, cols]), axis=1
        )
        packed[head, 2 * tokens :] = entries
        sends[head].start()
    for send in sends:
        send.wait()


def unpack_kernel(packed_ref, attended_ref, query_ref, key_ref, value_ref):
    tokens, width = key_ref.shape
    for head in range(width // HEAD_DIM):
        cols = slice(head * HEAD_DIM, (head + 1) * HEAD_DIM)
        first, second = packed_ref[head, :tokens], packed_ref[head, tokens:]
        query_ref[:, cols] = first[:, :HEAD_DIM]
        attended_ref[:, cols] = first[:, HEAD_DIM:]
        key_ref[:, cols] = second[:, :HEAD_DIM]
        value_ref[:, cols] = second[:, HEAD_DIM:]


def attend_kernel(
    pos_row_ref, pos_col_ref, x_ref, out_ref, acc, global_kv, global_acc, listed, starts, sem
):
    shards = out_ref.shape[0]
    tokens = out_ref.shape[1] // 2
    stride = x_ref.shape[0] // shards
    blocks = tokens // BLOCK
    global_count = pos_row_ref.shape[1]
    own = lax.axis_index("seq")

    lists = jnp.zeros(listed.shape, jnp.float32)
    list_lane = lax.broadcasted_iota(jnp.int32, listed.shape, 1)
    for shard in range(shards):
        row = x_ref[shard * stride + 2 * tokens : (shard + 1) * stride].astype(jnp.float32)
        entry = jnp.sum(jnp.where(list_lane == own, row, 0.0), axis=1, keepdims=True)
        lists = jnp.where(list_lane == shard, entry, lists)
    passed = jnp.floor((lists + 0.5) * (1.0 / blocks))
    listed[...] = (lists * BLOCK + passed * (stride - tokens)).astype(jnp.int32)
    copy = pltpu.make_async_copy(listed, starts, sem)
    copy.start()
    for shard in range(shards):
        acc[shard * stride : shard * stride + tokens] = jnp.zeros(
            (tokens, 2 * HEAD_DIM), jnp.float32
        )
    global_acc[...] = jnp.zeros_like(global_acc)
    picked = jnp.zeros((global_count, 2 * HEAD_DIM), jnp.float32)
    for shard in range(shards):
        place = shard * tokens + lax.broadcasted_iota(jnp.int32, (global_count, tokens), 1)
        pick = (place == pos_col_ref[...]).astype(jnp.bfloat16)
        picked = picked + dot(pick, x_ref[shard * stride : shard * stride + tokens], 1, 0)
    global_kv[...] = picked.astype(jnp.bfloat16)
    copy.wait()
    lane = lax.broadcasted_iota(jnp.int32, (BLOCK, 6 * BLOCK), 1)
    half = lax.broadcasted_iota(jnp.int32, (BLOCK, 2 * HEAD_DIM), 1) < HEAD_DIM
    query_mask = jnp.where(half, 1.0 / math.sqrt(HEAD_DIM), 0.0).astype(jnp.bfloat16)
    grad_mask = jnp.where(half, 0.0, 1.0).astype(jnp.bfloat16)

    def at(start):
        return pl.ds(pl.multiple_of(start, 16), BLOCK)

    def products(shard):
        base = shard * stride
        rows = []
        for block in range(blocks):
            rest = x_ref[at(base + tokens + block * BLOCK)]
            rows += [rest * query_mask, rest * grad_mask]
        rows = jnp.concatenate(rows, axis=0)
        all_places, local_kvs, local_dots = [], [], []
        for block in range(blocks):
            before = jnp.maximum(shard - 1, 0) * stride + (blocks - 1) * BLOCK
            after = jnp.minimum(shard + 1, shards - 1) * stride
            places = [
                base + (block - 1) * BLOCK if block else before,
                base + block * BLOCK,
                base + (block + 1) * BLOCK if block < blocks - 1 else after,
            ] + [starts[block * RAND + r, shard] for r in range(RAND)]
            all_places.append([at(p) for p in places])
            local_kvs.append(jnp.concatenate([x_ref[p] for p in all_places[-1]], axis=0))
            both = rows[2 * block * BLOCK : 2 * (block + 1) * BLOCK]
            local_dots.append(dot(both, local_kvs[-1], 1, 1))
        return rows, all_places, local_kvs, local_dots, dot(rows, global_kv[...], 1, 1)

    def weigh(shard, block, local_dots, global_dots):
        score, dp = local_dots[:BLOCK], local_dots[BLOCK:]
        if block == 0:
            score = jnp.where((lane < BLOCK) & (shard == 0), MASKED, score)
        if block == blocks - 1:
            outside = (lane >= 2 * BLOCK) & (lane < 3 * BLOCK)
            score = jnp.where(outside & (shard == shards - 1), MASKED, score)
        global_score, global_dp = global_dots[:BLOCK], global_dots[BLOCK:]
        highest = jnp.maximum(
            jnp.max(score, axis=1, keepdims=True),
            jnp.max(global_score, axis=1, keepdims=True),
        )
        local_exp = jnp.exp(score - highest)
        global_exp = jnp.exp(global_score - highest)
        inverse = 1.0 / (
            jnp.sum(local_exp, axis=1, keepdims=True)
            + jnp.sum(global_exp, axis=1, keepdims=True)
        )
        local_weight = (local_exp * inverse).astype(jnp.bfloat16)
        global_weight = (global_exp * inverse).astype(jnp.bfloat16)
        local_wf = local_weight.astype(jnp.float32)
        global_wf = global_weight.astype(jnp.float32)
        delta = jnp.sum(local_wf * dp, axis=1, keepdims=True) + jnp.sum(
            global_wf * global_dp, axis=1, keepdims=True
        )
        local_ds = (local_wf * (dp - delta)).astype(jnp.bfloat16)
        global_ds = (global_wf * (global_dp - delta)).astype(jnp.bfloat16)
        return (
            jnp.concatenate((local_ds, local_weight), axis=0),
            jnp.concatenate((global_ds, global_weight), axis=0),
        )

    def shard_group(group, carry):
        members = [group * GROUP + i for i in range(GROUP)]
        made = [products(shard) for shard in members]
        sides = [
            [
                weigh(
                    shard,
                    block,
                    local_dots[block],
                    global_dots[2 * block * BLOCK : 2 * (block + 1) * BLOCK],
                )
                for block in range(blocks)
            ]
            for shard, (_, _, _, local_dots, global_dots) in zip(members, made)
        ]
        gkv = global_kv[...]
        for shard, side, (rows, all_places, local_kvs, _, _) in zip(members, sides, made):
            global_side = jnp.concatenate([pair[1] for pair in side], axis=0)
            global_result = dot(global_side, gkv, 1, 0)
            results, grads = [], []
            for block in range(blocks):
                span = slice(2 * block * BLOCK, 2 * (block + 1) * BLOCK)
                results.append(dot(side[block][0], local_kvs[block], 1, 0) + global_result[span])
                grads.append(dot(side[block][0], rows[span], 0, 0))
            global_acc[...] += dot(global_side, rows, 0, 0)
            for block in range(blocks):
                out_ref[shard, block * BLOCK : (block + 1) * BLOCK] = jnp.where(
                    half,
                    results[block][:BLOCK] * (1.0 / math.sqrt(HEAD_DIM)),
                    results[block][BLOCK:],
                ).astype(jnp.bfloat16)
                for i, spot in enumerate(all_places[block]):
                    acc[spot] += grads[block][i * BLOCK : (i + 1) * BLOCK]
        return carry

    lax.fori_loop(0, shards // GROUP, shard_group, 0)
    global_grad = global_acc[...].astype(jnp.bfloat16)
    for shard in range(shards):
        place = shard * tokens + lax.broadcasted_iota(jnp.int32, (tokens, global_count), 0)
        spread = (place == pos_row_ref[...]).astype(jnp.bfloat16)
        out_ref[shard, tokens:] = (
            acc[shard * stride : shard * stride + tokens] + dot(spread, global_grad, 1, 0)
        ).astype(jnp.bfloat16)


def attend(whole, global_pos, tokens):
    shards, stride, pair = whole.shape
    lists = (stride - 2 * tokens, pair)
    global_count = global_pos.shape[0]
    return pl.pallas_call(
        attend_kernel,
        out_shape=jax.ShapeDtypeStruct((shards, 2 * tokens, pair), jnp.bfloat16),
        scratch_shapes=[
            pltpu.VMEM((shards * stride, pair), jnp.float32),
            pltpu.VMEM((global_count, pair), jnp.bfloat16),
            pltpu.VMEM((global_count, pair), jnp.float32),
            pltpu.VMEM(lists, jnp.int32),
            pltpu.SMEM(lists, jnp.int32),
            pltpu.SemaphoreType.DMA,
        ],
        compiler_params=pltpu.CompilerParams(vmem_limit_bytes=VMEM_BYTES),
    )(global_pos.reshape(1, -1), global_pos.reshape(-1, 1), whole.reshape(shards * stride, pair))


def whole_body(queries, key_input, value_input, grad_output, rand_blocks, global_pos):
    tokens, width = queries.shape
    shards = lax.axis_size("seq")
    extra = listed_rows(tokens)
    pair = 2 * HEAD_DIM
    slots = (shards, 2 * tokens + extra, pair)
    narrow = jax.ShapeDtypeStruct((tokens, width), jnp.bfloat16)
    anywhere = pl.BlockSpec(memory_space=pl.ANY)
    rand_lists = rand_blocks.transpose(0, 2, 1)
    packed = pl.pallas_call(
        pack_kernel,
        out_shape=jax.ShapeDtypeStruct(slots, jnp.bfloat16),
        in_specs=[anywhere] * 5,
        out_specs=anywhere,
        scratch_shapes=[pltpu.VMEM(rand_lists.shape, jnp.int32)]
        + [pltpu.VMEM((tokens, width), jnp.bfloat16)] * 4
        + [
            pltpu.VMEM((extra, pair), jnp.int32),
            pltpu.VMEM(slots, jnp.bfloat16),
            pltpu.SemaphoreType.DMA((5,)),
            pltpu.SemaphoreType.DMA((shards,)),
        ],
    )(rand_lists, key_input, value_input, queries, grad_output)
    whole = lax.all_to_all(packed, "seq", split_axis=0, concat_axis=0, tiled=True)
    result = attend(whole, global_pos, tokens)
    returned = lax.all_to_all(result, "seq", split_axis=0, concat_axis=0, tiled=True)
    return pl.pallas_call(
        unpack_kernel,
        out_shape=(narrow,) * 4,
        compiler_params=pltpu.CompilerParams(vmem_limit_bytes=VMEM_BYTES),
    )(returned)


def body(queries, *others):
    shards = lax.axis_size("seq")
    tokens, width = queries.shape
    if width // HEAD_DIM <= shards and shards * tokens <= WHOLE_ROWS:
        return whole_body(queries, *others)
    return sparse_body(queries, *others)


def solution(mesh):
    in_specs = (
        P(("groups", "seq"), "head"),
        P(("groups", "seq"), "head"),
        P(("groups", "seq"), "head"),
        P(("groups", "seq"), "head"),
        P(("groups", "seq"), "head", None),
        P("groups"),
    )
    out_specs = (
        P(("groups", "seq"), "head"),
        P(("groups", "seq"), "head"),
        P(("groups", "seq"), "head"),
        P(("groups", "seq"), "head"),
    )
    return jax.shard_map(body, mesh=mesh, in_specs=in_specs, out_specs=out_specs, check_vma=False)
```

```python
import math

import jax
import jax.numpy as jnp
from jax import lax
from jax.experimental import pallas as pl
from jax.experimental.pallas import tpu as pltpu
from jax.sharding import PartitionSpec as P

HEAD_DIM = 64
BLOCK = 64
RAND = 3


MASKED = -1e30


def with_halo(array, sides, width):
    for axis, dim in sides:
        size, length = (lax.axis_size(axis), array.shape[dim])
        up = [(i, (i + 1) % size) for i in range(size - 1)]
        down = [(j, i) for i, j in up]
        last = lax.slice_in_dim(array, length - width, length, axis=dim)
        initial = lax.slice_in_dim(array, 0, width, axis=dim)
        before = lax.ppermute(last, axis, up)
        after = lax.ppermute(initial, axis, down)
        array = jnp.concatenate([before, array, after], axis=dim)
    return array


def attend_head(
    query, key_rows, value_rows, visible, global_keys, global_values, grad_out, score_scale
):
    local_score = (
        jnp.einsum("nqe,nke->nqk", query, key_rows, preferred_element_type=jnp.float32)
        * score_scale
    )
    local_score = jnp.where(visible, local_score, MASKED)
    global_score = (
        jnp.einsum("nqe,ke->nqk", query, global_keys, preferred_element_type=jnp.float32)
        * score_scale
    )
    highest = jnp.maximum(
        jnp.max(local_score, axis=-1, keepdims=True), jnp.max(global_score, axis=-1, keepdims=True)
    )
    local_exp = jnp.exp(local_score - highest)
    global_exp = jnp.exp(global_score - highest)
    totals = jnp.sum(local_exp, axis=-1, keepdims=True) + jnp.sum(
        global_exp, axis=-1, keepdims=True
    )
    local_weight = (local_exp / totals).astype(jnp.bfloat16)
    global_weight = (global_exp / totals).astype(jnp.bfloat16)
    outputs = (
        jnp.einsum("nqk,nke->nqe", local_weight, value_rows, preferred_element_type=jnp.float32)
        + jnp.einsum(
            "nqk,ke->nqe", global_weight, global_values, preferred_element_type=jnp.float32
        )
    ).astype(jnp.bfloat16)
    local_dp = jnp.einsum("nqe,nke->nqk", grad_out, value_rows, preferred_element_type=jnp.float32)
    global_dp = jnp.einsum(
        "nqe,ke->nqk", grad_out, global_values, preferred_element_type=jnp.float32
    )
    local_wf = local_weight.astype(jnp.float32)
    global_wf = global_weight.astype(jnp.float32)
    delta_sum = jnp.sum(local_wf * local_dp, axis=-1, keepdims=True) + jnp.sum(
        global_wf * global_dp, axis=-1, keepdims=True
    )
    local_ds = (local_wf * (local_dp - delta_sum) * score_scale).astype(jnp.bfloat16)
    global_ds = (global_wf * (global_dp - delta_sum) * score_scale).astype(jnp.bfloat16)
    grad_query = (
        jnp.einsum("nqk,nke->nqe", local_ds, key_rows, preferred_element_type=jnp.float32)
        + jnp.einsum("nqk,ke->nqe", global_ds, global_keys, preferred_element_type=jnp.float32)
    ).astype(jnp.bfloat16)
    local_dk = jnp.einsum("nqk,nqe->nke", local_ds, query, preferred_element_type=jnp.float32)
    local_dv = jnp.einsum(
        "nqk,nqe->nke", local_weight, grad_out, preferred_element_type=jnp.float32
    )
    global_dk = jnp.einsum("nqk,nqe->ke", global_ds, query, preferred_element_type=jnp.float32)
    global_dv = jnp.einsum(
        "nqk,nqe->ke", global_weight, grad_out, preferred_element_type=jnp.float32
    )
    return (outputs, grad_query, local_dk, local_dv, global_dk, global_dv, local_ds, local_weight)


def sparse_body(queries, key_input, value_input, grad_output, rand_blocks, global_pos):
    tokens = queries.shape[0]
    blocks = tokens // BLOCK
    head_count = queries.shape[1] // HEAD_DIM
    pair_width = 2 * HEAD_DIM
    shards = lax.axis_size("seq")
    own_index = lax.axis_index("seq")
    first_row = own_index * tokens
    score_scale = 1.0 / math.sqrt(HEAD_DIM)
    packed_kv = jnp.concatenate(
        (
            key_input.reshape(tokens, head_count, HEAD_DIM),
            value_input.reshape(tokens, head_count, HEAD_DIM),
        ),
        axis=2,
    )
    padded = with_halo(packed_kv, (("seq", 0),), BLOCK)
    window_kv = jnp.concatenate(
        [
            padded[offset * BLOCK : offset * BLOCK + tokens].reshape(
                blocks, BLOCK, head_count, pair_width
            )
            for offset in range(3)
        ],
        axis=1,
    ).transpose(2, 0, 1, 3)
    request_block = rand_blocks.reshape(-1)
    requests = request_block.shape[0]
    request_ids = jnp.arange(requests, dtype=jnp.int32)
    request_head = request_ids // RAND % head_count
    owner_shard = request_block // blocks
    capacity = max(2, (requests + shards - 1) // shards)
    slots_all = shards * capacity
    earlier = (owner_shard[:, None] == owner_shard[None, :]) & (
        request_ids[None, :] < request_ids[:, None]
    )
    slot_rank = jnp.sum(earlier.astype(jnp.int32), axis=1)
    request_slot = owner_shard * capacity + slot_rank
    slot_match = request_slot[None, :] == jnp.arange(slots_all, dtype=jnp.int32)[:, None]
    slot_used = jnp.any(slot_match, axis=1)
    slot_source = jnp.sum(jnp.where(slot_match, request_ids[None, :], 0), axis=1)
    request_code = request_block % blocks * head_count + request_head
    wanted = jnp.where(slot_used, jnp.take(request_code, slot_source), -1).reshape(shards, capacity)
    block_table = (
        packed_kv.reshape(blocks, BLOCK, head_count, pair_width)
        .transpose(0, 2, 1, 3)
        .reshape(blocks * head_count, BLOCK, pair_width)
    )
    asked_codes = lax.all_to_all(wanted, "seq", split_axis=0, concat_axis=0, tiled=True)
    picked = jnp.take(block_table, jnp.maximum(asked_codes, 0), axis=0)
    fetched, asked_codes = (
        lax.all_to_all(picked, "seq", split_axis=0, concat_axis=0, tiled=True),
        asked_codes,
    )
    random_kv = jnp.take(fetched.reshape(slots_all, BLOCK, pair_width), request_slot, axis=0)
    random_kv = random_kv.reshape(blocks, head_count, RAND * BLOCK, pair_width).transpose(
        1, 0, 2, 3
    )
    local_kv = jnp.concatenate((window_kv, random_kv), axis=2)
    block_ids = own_index * blocks + jnp.arange(blocks, dtype=jnp.int32)
    neighbour = block_ids[:, None] + jnp.arange(3, dtype=jnp.int32)[None, :] - 1
    inside = (neighbour >= 0) & (neighbour < blocks * shards)
    visible = jnp.concatenate(
        (jnp.repeat(inside, BLOCK, axis=1), jnp.ones((blocks, RAND * BLOCK), jnp.bool_)), axis=1
    )[:, None, :]
    global_count = global_pos.shape[0]
    global_ids = jnp.arange(global_count, dtype=jnp.int32)
    row_ids = jnp.arange(tokens, dtype=jnp.int32)
    flat_kv = packed_kv.reshape(tokens, head_count * pair_width)
    row_match = global_pos[:, None] == first_row + row_ids[None, :]
    partial_rows = jnp.dot(
        row_match.astype(jnp.bfloat16), flat_kv, preferred_element_type=jnp.float32
    )
    global_kv = lax.psum(partial_rows, "seq").astype(jnp.bfloat16)
    global_kv = global_kv.reshape(global_count, head_count, pair_width).transpose(1, 0, 2)

    def heads_first(array):
        return array.reshape(blocks, BLOCK, head_count, HEAD_DIM).transpose(2, 0, 1, 3)

    query_heads = heads_first(queries)
    grad_heads = heads_first(grad_output)

    def one_head(operands):
        query, local_pair, global_pair, grad_out = operands
        return attend_head(
            query,
            local_pair[..., :HEAD_DIM],
            local_pair[..., HEAD_DIM:],
            visible,
            global_pair[:, :HEAD_DIM],
            global_pair[:, HEAD_DIM:],
            grad_out,
            score_scale,
        )

    outputs, grad_query, local_dk, local_dv, global_dk, global_dv, local_ds, local_weight = lax.map(
        one_head, (query_heads, local_kv, global_kv, grad_heads)
    )

    def rows_last(array):
        return array.transpose(1, 2, 0, 3).reshape(tokens, head_count * HEAD_DIM)

    local_grad = jnp.concatenate((local_dk, local_dv), axis=3)
    window_grad = local_grad[:, :, : 3 * BLOCK].transpose(1, 2, 0, 3)
    spread = sum(
        (
            jnp.pad(
                window_grad[:, offset * BLOCK : (offset + 1) * BLOCK].reshape(
                    tokens, head_count, pair_width
                ),
                ((offset * BLOCK, (2 - offset) * BLOCK), (0, 0), (0, 0)),
            )
            for offset in range(3)
        )
    )
    rim_pair = jnp.concatenate((spread[:BLOCK], spread[-BLOCK:]), axis=0)
    rim_in = with_halo(rim_pair.astype(jnp.bfloat16), (("seq", 0),), BLOCK).astype(rim_pair.dtype)
    window_total = (
        spread[BLOCK:-BLOCK]
        + jnp.pad(rim_in[:BLOCK], ((0, tokens - BLOCK), (0, 0), (0, 0)))
        + jnp.pad(rim_in[-BLOCK:], ((tokens - BLOCK, 0), (0, 0), (0, 0)))
    )
    random_grad = local_grad[:, :, 3 * BLOCK :].reshape(head_count, blocks, RAND, BLOCK, pair_width)
    random_grad = (
        random_grad.transpose(1, 0, 2, 3, 4)
        .reshape(requests, BLOCK, pair_width)
        .astype(jnp.bfloat16)
    )
    outgoing = jnp.where(slot_used[:, None, None], jnp.take(random_grad, slot_source, axis=0), 0)
    returned = lax.all_to_all(
        outgoing.reshape(shards, capacity, BLOCK, pair_width),
        "seq",
        split_axis=0,
        concat_axis=0,
        tiled=True,
    )
    target = (
        asked_codes.reshape(-1)[None, :]
        == jnp.arange(blocks * head_count, dtype=jnp.int32)[:, None]
    ).astype(jnp.bfloat16)
    random_total = jnp.dot(
        target, returned.reshape(slots_all, BLOCK * pair_width), preferred_element_type=jnp.float32
    )
    random_total = (
        random_total.reshape(blocks, head_count, BLOCK, pair_width)
        .transpose(0, 2, 1, 3)
        .reshape(tokens, head_count, pair_width)
    )
    global_grad = (
        jnp.concatenate((global_dk, global_dv), axis=2)
        .transpose(1, 0, 2)
        .reshape(global_count, head_count * pair_width)
    )
    global_total = lax.psum(global_grad, "seq")
    row_source = jnp.sum(jnp.where(row_match, global_ids[:, None], 0), axis=0)
    row_used = jnp.any(row_match, axis=0)
    global_rows = jnp.where(row_used[:, None], jnp.take(global_total, row_source, axis=0), 0.0)
    grand_total = window_total + random_total + global_rows.reshape(tokens, head_count, pair_width)
    key_rows_out = (
        grand_total[..., :HEAD_DIM].reshape(tokens, head_count * HEAD_DIM).astype(jnp.bfloat16)
    )
    value_rows_out = (
        grand_total[..., HEAD_DIM:].reshape(tokens, head_count * HEAD_DIM).astype(jnp.bfloat16)
    )
    return (rows_last(outputs), rows_last(grad_query), key_rows_out, value_rows_out)


WHOLE_ROWS = 4096
GROUP = 4
VMEM_BYTES = 32 * 1024 * 1024


def dot(left, right, left_dim, right_dim):
    return lax.dot_general(
        left,
        right,
        (((left_dim,), (right_dim,)), ((), ())),
        preferred_element_type=jnp.float32,
    )


def listed_rows(tokens):
    return -(-(tokens // BLOCK * RAND) // 16) * 16


def pack_kernel(rand_hbm, key_hbm, value_hbm, query_hbm, grad_hbm, packed_hbm, *scratch):
    *targets, listed, packed, sems, out_sems = scratch
    rand_ref, key_ref, value_ref, query_ref, grad_ref = targets
    tokens, width = key_ref.shape
    heads = width // HEAD_DIM
    slots = packed.shape[0]
    copies = [
        pltpu.make_async_copy(source, target, sems.at[i])
        for i, (source, target) in enumerate(
            zip((rand_hbm, key_hbm, value_hbm, query_hbm, grad_hbm), targets)
        )
    ]
    sends = [
        pltpu.make_async_copy(packed.at[slot], packed_hbm.at[slot], out_sems.at[slot])
        for slot in range(slots)
    ]
    for copy in copies:
        copy.start()
    listed[...] = jnp.zeros_like(listed)
    for slot in range(heads, slots):
        packed[slot] = jnp.zeros(packed.shape[1:], jnp.bfloat16)
        sends[slot].start()
    for copy in copies:
        copy.wait()
    for block in range(tokens // BLOCK):
        listed[block * RAND : (block + 1) * RAND, :heads] = rand_ref[block]
    entries = listed[...].astype(jnp.float32).astype(jnp.bfloat16)
    for head in range(heads):
        cols = slice(head * HEAD_DIM, (head + 1) * HEAD_DIM)
        packed[head, :tokens] = jnp.concatenate((key_ref[:, cols], value_ref[:, cols]), axis=1)
        packed[head, tokens : 2 * tokens] = jnp.concatenate(
            (query_ref[:, cols], grad_ref[:, cols]), axis=1
        )
        packed[head, 2 * tokens :] = entries
        sends[head].start()
    for send in sends:
        send.wait()


def unpack_kernel(packed_ref, attended_ref, query_ref, key_ref, value_ref):
    tokens, width = key_ref.shape
    for head in range(width // HEAD_DIM):
        cols = slice(head * HEAD_DIM, (head + 1) * HEAD_DIM)
        first, second = packed_ref[head, :tokens], packed_ref[head, tokens:]
        query_ref[:, cols] = first[:, :HEAD_DIM]
        attended_ref[:, cols] = first[:, HEAD_DIM:]
        key_ref[:, cols] = second[:, :HEAD_DIM]
        value_ref[:, cols] = second[:, HEAD_DIM:]


def places_kernel(pos_row_ref, pos_col_ref, pick_ref, spread_ref):
    position = lax.broadcasted_iota(jnp.int32, pick_ref.shape, 1)
    pick_ref[...] = (position == pos_col_ref[...]).astype(jnp.bfloat16)
    position = lax.broadcasted_iota(jnp.int32, spread_ref.shape, 0)
    spread_ref[...] = (position == pos_row_ref[...]).astype(jnp.bfloat16)


def attend_kernel(
    pick_ref, spread_ref, x_ref, out_ref, acc, global_kv, global_acc, listed, starts, sem
):
    shards = out_ref.shape[0]
    tokens = out_ref.shape[1] // 2
    stride = x_ref.shape[0] // shards
    blocks = tokens // BLOCK
    own = lax.axis_index("seq")

    lists = jnp.zeros(listed.shape, jnp.float32)
    list_lane = lax.broadcasted_iota(jnp.int32, listed.shape, 1)
    for shard in range(shards):
        row = x_ref[shard * stride + 2 * tokens : (shard + 1) * stride].astype(jnp.float32)
        entry = jnp.sum(jnp.where(list_lane == own, row, 0.0), axis=1, keepdims=True)
        lists = jnp.where(list_lane == shard, entry, lists)
    passed = jnp.floor((lists + 0.5) * (1.0 / blocks))
    listed[...] = (lists * BLOCK + passed * (stride - tokens)).astype(jnp.int32)
    copy = pltpu.make_async_copy(listed, starts, sem)
    copy.start()
    for shard in range(shards):
        acc[shard * stride : shard * stride + tokens] = jnp.zeros(
            (tokens, 2 * HEAD_DIM), jnp.float32
        )
    global_acc[...] = jnp.zeros_like(global_acc)
    all_kv = jnp.concatenate(
        [x_ref[shard * stride : shard * stride + tokens] for shard in range(shards)], axis=0
    )
    global_kv[...] = dot(pick_ref[...], all_kv, 1, 0).astype(jnp.bfloat16)
    copy.wait()
    lane = lax.broadcasted_iota(jnp.int32, (BLOCK, 6 * BLOCK), 1)
    half = lax.broadcasted_iota(jnp.int32, (BLOCK, 2 * HEAD_DIM), 1) < HEAD_DIM
    query_mask = jnp.where(half, 1.0 / math.sqrt(HEAD_DIM), 0.0).astype(jnp.bfloat16)
    grad_mask = jnp.where(half, 0.0, 1.0).astype(jnp.bfloat16)

    def at(start):
        return pl.ds(pl.multiple_of(start, 16), BLOCK)

    def products(shard):
        base = shard * stride
        rows = []
        for block in range(blocks):
            rest = x_ref[at(base + tokens + block * BLOCK)]
            rows += [rest * query_mask, rest * grad_mask]
        rows = jnp.concatenate(rows, axis=0)
        all_places, local_kvs, local_dots = [], [], []
        for block in range(blocks):
            before = jnp.maximum(shard - 1, 0) * stride + (blocks - 1) * BLOCK
            after = jnp.minimum(shard + 1, shards - 1) * stride
            places = [
                base + (block - 1) * BLOCK if block else before,
                base + block * BLOCK,
                base + (block + 1) * BLOCK if block < blocks - 1 else after,
            ] + [starts[block * RAND + r, shard] for r in range(RAND)]
            all_places.append([at(p) for p in places])
            local_kvs.append(jnp.concatenate([x_ref[p] for p in all_places[-1]], axis=0))
            both = rows[2 * block * BLOCK : 2 * (block + 1) * BLOCK]
            local_dots.append(dot(both, local_kvs[-1], 1, 1))
        return rows, all_places, local_kvs, local_dots, dot(rows, global_kv[...], 1, 1)

    def weigh(shard, block, local_dots, global_dots):
        score, dp = local_dots[:BLOCK], local_dots[BLOCK:]
        if block == 0:
            score = jnp.where((lane < BLOCK) & (shard == 0), MASKED, score)
        if block == blocks - 1:
            outside = (lane >= 2 * BLOCK) & (lane < 3 * BLOCK)
            score = jnp.where(outside & (shard == shards - 1), MASKED, score)
        global_score, global_dp = global_dots[:BLOCK], global_dots[BLOCK:]
        highest = jnp.maximum(
            jnp.max(score, axis=1, keepdims=True),
            jnp.max(global_score, axis=1, keepdims=True),
        )
        local_exp = jnp.exp(score - highest)
        global_exp = jnp.exp(global_score - highest)
        inverse = 1.0 / (
            jnp.sum(local_exp, axis=1, keepdims=True)
            + jnp.sum(global_exp, axis=1, keepdims=True)
        )
        local_weight = (local_exp * inverse).astype(jnp.bfloat16)
        global_weight = (global_exp * inverse).astype(jnp.bfloat16)
        local_wf = local_weight.astype(jnp.float32)
        global_wf = global_weight.astype(jnp.float32)
        delta = jnp.sum(local_wf * dp, axis=1, keepdims=True) + jnp.sum(
            global_wf * global_dp, axis=1, keepdims=True
        )
        local_ds = (local_wf * (dp - delta)).astype(jnp.bfloat16)
        global_ds = (global_wf * (global_dp - delta)).astype(jnp.bfloat16)
        return (
            jnp.concatenate((local_ds, local_weight), axis=0),
            jnp.concatenate((global_ds, global_weight), axis=0),
        )

    def shard_group(group, carry):
        members = [group * GROUP + i for i in range(GROUP)]
        made = [products(shard) for shard in members]
        sides = [
            [
                weigh(
                    shard,
                    block,
                    local_dots[block],
                    global_dots[2 * block * BLOCK : 2 * (block + 1) * BLOCK],
                )
                for block in range(blocks)
            ]
            for shard, (_, _, _, local_dots, global_dots) in zip(members, made)
        ]
        gkv = global_kv[...]
        for shard, side, (rows, all_places, local_kvs, _, _) in zip(members, sides, made):
            global_side = jnp.concatenate([pair[1] for pair in side], axis=0)
            global_result = dot(global_side, gkv, 1, 0)
            results, grads = [], []
            for block in range(blocks):
                span = slice(2 * block * BLOCK, 2 * (block + 1) * BLOCK)
                results.append(dot(side[block][0], local_kvs[block], 1, 0) + global_result[span])
                grads.append(dot(side[block][0], rows[span], 0, 0))
            global_acc[...] += dot(rows, global_side, 0, 0)
            for block in range(blocks):
                out_ref[shard, block * BLOCK : (block + 1) * BLOCK] = jnp.where(
                    half,
                    results[block][:BLOCK] * (1.0 / math.sqrt(HEAD_DIM)),
                    results[block][BLOCK:],
                ).astype(jnp.bfloat16)
                for i, spot in enumerate(all_places[block]):
                    acc[spot] += grads[block][i * BLOCK : (i + 1) * BLOCK]
        return carry

    lax.fori_loop(0, shards // GROUP, shard_group, 0)
    global_grad = global_acc[...].astype(jnp.bfloat16)
    for shard in range(shards):
        spread = spread_ref[shard * tokens : (shard + 1) * tokens]
        out_ref[shard, tokens:] = (
            acc[shard * stride : shard * stride + tokens] + dot(spread, global_grad, 1, 1)
        ).astype(jnp.bfloat16)


def attend(whole, global_pos, tokens):
    shards, stride, pair = whole.shape
    lists = (stride - 2 * tokens, pair)
    global_count = global_pos.shape[0]
    pick, spread = pl.pallas_call(
        places_kernel,
        out_shape=(
            jax.ShapeDtypeStruct((global_count, shards * tokens), jnp.bfloat16),
            jax.ShapeDtypeStruct((shards * tokens, global_count), jnp.bfloat16),
        ),
        compiler_params=pltpu.CompilerParams(vmem_limit_bytes=VMEM_BYTES),
        cost_estimate=pl.CostEstimate(
            flops=4 * shards * tokens * global_count,
            bytes_accessed=4 * shards * tokens * global_count,
            transcendentals=0,
        ),
    )(global_pos.reshape(1, -1), global_pos.reshape(-1, 1))
    return pl.pallas_call(
        attend_kernel,
        out_shape=jax.ShapeDtypeStruct((shards, 2 * tokens, pair), jnp.bfloat16),
        scratch_shapes=[
            pltpu.VMEM((shards * stride, pair), jnp.float32),
            pltpu.VMEM((global_count, pair), jnp.bfloat16),
            pltpu.VMEM((pair, global_count), jnp.float32),
            pltpu.VMEM(lists, jnp.int32),
            pltpu.SMEM(lists, jnp.int32),
            pltpu.SemaphoreType.DMA,
        ],
        compiler_params=pltpu.CompilerParams(vmem_limit_bytes=VMEM_BYTES),
    )(pick, spread, whole.reshape(shards * stride, pair))


def whole_body(queries, key_input, value_input, grad_output, rand_blocks, global_pos):
    tokens, width = queries.shape
    shards = lax.axis_size("seq")
    extra = listed_rows(tokens)
    pair = 2 * HEAD_DIM
    slots = (shards, 2 * tokens + extra, pair)
    narrow = jax.ShapeDtypeStruct((tokens, width), jnp.bfloat16)
    anywhere = pl.BlockSpec(memory_space=pl.ANY)
    rand_lists = rand_blocks.transpose(0, 2, 1)
    packed = pl.pallas_call(
        pack_kernel,
        out_shape=jax.ShapeDtypeStruct(slots, jnp.bfloat16),
        in_specs=[anywhere] * 5,
        out_specs=anywhere,
        scratch_shapes=[pltpu.VMEM(rand_lists.shape, jnp.int32)]
        + [pltpu.VMEM((tokens, width), jnp.bfloat16)] * 4
        + [
            pltpu.VMEM((extra, pair), jnp.int32),
            pltpu.VMEM(slots, jnp.bfloat16),
            pltpu.SemaphoreType.DMA((5,)),
            pltpu.SemaphoreType.DMA((shards,)),
        ],
    )(rand_lists, key_input, value_input, queries, grad_output)
    whole = lax.all_to_all(packed, "seq", split_axis=0, concat_axis=0, tiled=True)
    result = attend(whole, global_pos, tokens)
    returned = lax.all_to_all(result, "seq", split_axis=0, concat_axis=0, tiled=True)
    return pl.pallas_call(
        unpack_kernel,
        out_shape=(narrow,) * 4,
        compiler_params=pltpu.CompilerParams(vmem_limit_bytes=VMEM_BYTES),
    )(returned)


def body(queries, *others):
    shards = lax.axis_size("seq")
    tokens, width = queries.shape
    if width // HEAD_DIM <= shards and shards * tokens <= WHOLE_ROWS:
        return whole_body(queries, *others)
    return sparse_body(queries, *others)


def solution(mesh):
    in_specs = (
        P(("groups", "seq"), "head"),
        P(("groups", "seq"), "head"),
        P(("groups", "seq"), "head"),
        P(("groups", "seq"), "head"),
        P(("groups", "seq"), "head", None),
        P("groups"),
    )
    out_specs = (
        P(("groups", "seq"), "head"),
        P(("groups", "seq"), "head"),
        P(("groups", "seq"), "head"),
        P(("groups", "seq"), "head"),
    )
    return jax.shard_map(body, mesh=mesh, in_specs=in_specs, out_specs=out_specs, check_vma=False)
```

```python
import math

import jax
import jax.numpy as jnp
from jax import lax
from jax.experimental import pallas as pl
from jax.experimental.pallas import tpu as pltpu
from jax.sharding import PartitionSpec as P

HEAD_DIM = 64
BLOCK = 64
RAND = 3


MASKED = -1e30


def with_halo(array, sides, width):
    for axis, dim in sides:
        size, length = (lax.axis_size(axis), array.shape[dim])
        up = [(i, (i + 1) % size) for i in range(size - 1)]
        down = [(j, i) for i, j in up]
        last = lax.slice_in_dim(array, length - width, length, axis=dim)
        initial = lax.slice_in_dim(array, 0, width, axis=dim)
        before = lax.ppermute(last, axis, up)
        after = lax.ppermute(initial, axis, down)
        array = jnp.concatenate([before, array, after], axis=dim)
    return array


def attend_head(
    query, key_rows, value_rows, visible, global_keys, global_values, grad_out, score_scale
):
    local_score = (
        jnp.einsum("nqe,nke->nqk", query, key_rows, preferred_element_type=jnp.float32)
        * score_scale
    )
    local_score = jnp.where(visible, local_score, MASKED)
    global_score = (
        jnp.einsum("nqe,ke->nqk", query, global_keys, preferred_element_type=jnp.float32)
        * score_scale
    )
    highest = jnp.maximum(
        jnp.max(local_score, axis=-1, keepdims=True), jnp.max(global_score, axis=-1, keepdims=True)
    )
    local_exp = jnp.exp(local_score - highest)
    global_exp = jnp.exp(global_score - highest)
    totals = jnp.sum(local_exp, axis=-1, keepdims=True) + jnp.sum(
        global_exp, axis=-1, keepdims=True
    )
    local_weight = (local_exp / totals).astype(jnp.bfloat16)
    global_weight = (global_exp / totals).astype(jnp.bfloat16)
    outputs = (
        jnp.einsum("nqk,nke->nqe", local_weight, value_rows, preferred_element_type=jnp.float32)
        + jnp.einsum(
            "nqk,ke->nqe", global_weight, global_values, preferred_element_type=jnp.float32
        )
    ).astype(jnp.bfloat16)
    local_dp = jnp.einsum("nqe,nke->nqk", grad_out, value_rows, preferred_element_type=jnp.float32)
    global_dp = jnp.einsum(
        "nqe,ke->nqk", grad_out, global_values, preferred_element_type=jnp.float32
    )
    local_wf = local_weight.astype(jnp.float32)
    global_wf = global_weight.astype(jnp.float32)
    delta_sum = jnp.sum(local_wf * local_dp, axis=-1, keepdims=True) + jnp.sum(
        global_wf * global_dp, axis=-1, keepdims=True
    )
    local_ds = (local_wf * (local_dp - delta_sum) * score_scale).astype(jnp.bfloat16)
    global_ds = (global_wf * (global_dp - delta_sum) * score_scale).astype(jnp.bfloat16)
    grad_query = (
        jnp.einsum("nqk,nke->nqe", local_ds, key_rows, preferred_element_type=jnp.float32)
        + jnp.einsum("nqk,ke->nqe", global_ds, global_keys, preferred_element_type=jnp.float32)
    ).astype(jnp.bfloat16)
    local_dk = jnp.einsum("nqk,nqe->nke", local_ds, query, preferred_element_type=jnp.float32)
    local_dv = jnp.einsum(
        "nqk,nqe->nke", local_weight, grad_out, preferred_element_type=jnp.float32
    )
    global_dk = jnp.einsum("nqk,nqe->ke", global_ds, query, preferred_element_type=jnp.float32)
    global_dv = jnp.einsum(
        "nqk,nqe->ke", global_weight, grad_out, preferred_element_type=jnp.float32
    )
    return (outputs, grad_query, local_dk, local_dv, global_dk, global_dv, local_ds, local_weight)


def sparse_body(queries, key_input, value_input, grad_output, rand_blocks, global_pos):
    tokens = queries.shape[0]
    blocks = tokens // BLOCK
    head_count = queries.shape[1] // HEAD_DIM
    pair_width = 2 * HEAD_DIM
    shards = lax.axis_size("seq")
    own_index = lax.axis_index("seq")
    first_row = own_index * tokens
    score_scale = 1.0 / math.sqrt(HEAD_DIM)
    packed_kv = jnp.concatenate(
        (
            key_input.reshape(tokens, head_count, HEAD_DIM),
            value_input.reshape(tokens, head_count, HEAD_DIM),
        ),
        axis=2,
    )
    padded = with_halo(packed_kv, (("seq", 0),), BLOCK)
    window_kv = jnp.concatenate(
        [
            padded[offset * BLOCK : offset * BLOCK + tokens].reshape(
                blocks, BLOCK, head_count, pair_width
            )
            for offset in range(3)
        ],
        axis=1,
    ).transpose(2, 0, 1, 3)
    request_block = rand_blocks.reshape(-1)
    requests = request_block.shape[0]
    request_ids = jnp.arange(requests, dtype=jnp.int32)
    request_head = request_ids // RAND % head_count
    owner_shard = request_block // blocks
    capacity = max(2, (requests + shards - 1) // shards)
    slots_all = shards * capacity
    earlier = (owner_shard[:, None] == owner_shard[None, :]) & (
        request_ids[None, :] < request_ids[:, None]
    )
    slot_rank = jnp.sum(earlier.astype(jnp.int32), axis=1)
    request_slot = owner_shard * capacity + slot_rank
    slot_match = request_slot[None, :] == jnp.arange(slots_all, dtype=jnp.int32)[:, None]
    slot_used = jnp.any(slot_match, axis=1)
    slot_source = jnp.sum(jnp.where(slot_match, request_ids[None, :], 0), axis=1)
    request_code = request_block % blocks * head_count + request_head
    wanted = jnp.where(slot_used, jnp.take(request_code, slot_source), -1).reshape(shards, capacity)
    block_table = (
        packed_kv.reshape(blocks, BLOCK, head_count, pair_width)
        .transpose(0, 2, 1, 3)
        .reshape(blocks * head_count, BLOCK, pair_width)
    )
    asked_codes = lax.all_to_all(wanted, "seq", split_axis=0, concat_axis=0, tiled=True)
    picked = jnp.take(block_table, jnp.maximum(asked_codes, 0), axis=0)
    fetched, asked_codes = (
        lax.all_to_all(picked, "seq", split_axis=0, concat_axis=0, tiled=True),
        asked_codes,
    )
    random_kv = jnp.take(fetched.reshape(slots_all, BLOCK, pair_width), request_slot, axis=0)
    random_kv = random_kv.reshape(blocks, head_count, RAND * BLOCK, pair_width).transpose(
        1, 0, 2, 3
    )
    local_kv = jnp.concatenate((window_kv, random_kv), axis=2)
    block_ids = own_index * blocks + jnp.arange(blocks, dtype=jnp.int32)
    neighbour = block_ids[:, None] + jnp.arange(3, dtype=jnp.int32)[None, :] - 1
    inside = (neighbour >= 0) & (neighbour < blocks * shards)
    visible = jnp.concatenate(
        (jnp.repeat(inside, BLOCK, axis=1), jnp.ones((blocks, RAND * BLOCK), jnp.bool_)), axis=1
    )[:, None, :]
    global_count = global_pos.shape[0]
    global_ids = jnp.arange(global_count, dtype=jnp.int32)
    row_ids = jnp.arange(tokens, dtype=jnp.int32)
    flat_kv = packed_kv.reshape(tokens, head_count * pair_width)
    row_match = global_pos[:, None] == first_row + row_ids[None, :]
    partial_rows = jnp.dot(
        row_match.astype(jnp.bfloat16), flat_kv, preferred_element_type=jnp.float32
    )
    global_kv = lax.psum(partial_rows, "seq").astype(jnp.bfloat16)
    global_kv = global_kv.reshape(global_count, head_count, pair_width).transpose(1, 0, 2)

    def heads_first(array):
        return array.reshape(blocks, BLOCK, head_count, HEAD_DIM).transpose(2, 0, 1, 3)

    query_heads = heads_first(queries)
    grad_heads = heads_first(grad_output)

    def one_head(operands):
        query, local_pair, global_pair, grad_out = operands
        return attend_head(
            query,
            local_pair[..., :HEAD_DIM],
            local_pair[..., HEAD_DIM:],
            visible,
            global_pair[:, :HEAD_DIM],
            global_pair[:, HEAD_DIM:],
            grad_out,
            score_scale,
        )

    outputs, grad_query, local_dk, local_dv, global_dk, global_dv, local_ds, local_weight = lax.map(
        one_head, (query_heads, local_kv, global_kv, grad_heads)
    )

    def rows_last(array):
        return array.transpose(1, 2, 0, 3).reshape(tokens, head_count * HEAD_DIM)

    local_grad = jnp.concatenate((local_dk, local_dv), axis=3)
    window_grad = local_grad[:, :, : 3 * BLOCK].transpose(1, 2, 0, 3)
    spread = sum(
        (
            jnp.pad(
                window_grad[:, offset * BLOCK : (offset + 1) * BLOCK].reshape(
                    tokens, head_count, pair_width
                ),
                ((offset * BLOCK, (2 - offset) * BLOCK), (0, 0), (0, 0)),
            )
            for offset in range(3)
        )
    )
    rim_pair = jnp.concatenate((spread[:BLOCK], spread[-BLOCK:]), axis=0)
    rim_in = with_halo(rim_pair.astype(jnp.bfloat16), (("seq", 0),), BLOCK).astype(rim_pair.dtype)
    window_total = (
        spread[BLOCK:-BLOCK]
        + jnp.pad(rim_in[:BLOCK], ((0, tokens - BLOCK), (0, 0), (0, 0)))
        + jnp.pad(rim_in[-BLOCK:], ((tokens - BLOCK, 0), (0, 0), (0, 0)))
    )
    random_grad = local_grad[:, :, 3 * BLOCK :].reshape(head_count, blocks, RAND, BLOCK, pair_width)
    random_grad = (
        random_grad.transpose(1, 0, 2, 3, 4)
        .reshape(requests, BLOCK, pair_width)
        .astype(jnp.bfloat16)
    )
    outgoing = jnp.where(slot_used[:, None, None], jnp.take(random_grad, slot_source, axis=0), 0)
    returned = lax.all_to_all(
        outgoing.reshape(shards, capacity, BLOCK, pair_width),
        "seq",
        split_axis=0,
        concat_axis=0,
        tiled=True,
    )
    target = (
        asked_codes.reshape(-1)[None, :]
        == jnp.arange(blocks * head_count, dtype=jnp.int32)[:, None]
    ).astype(jnp.bfloat16)
    random_total = jnp.dot(
        target, returned.reshape(slots_all, BLOCK * pair_width), preferred_element_type=jnp.float32
    )
    random_total = (
        random_total.reshape(blocks, head_count, BLOCK, pair_width)
        .transpose(0, 2, 1, 3)
        .reshape(tokens, head_count, pair_width)
    )
    global_grad = (
        jnp.concatenate((global_dk, global_dv), axis=2)
        .transpose(1, 0, 2)
        .reshape(global_count, head_count * pair_width)
    )
    global_total = lax.psum(global_grad, "seq")
    row_source = jnp.sum(jnp.where(row_match, global_ids[:, None], 0), axis=0)
    row_used = jnp.any(row_match, axis=0)
    global_rows = jnp.where(row_used[:, None], jnp.take(global_total, row_source, axis=0), 0.0)
    grand_total = window_total + random_total + global_rows.reshape(tokens, head_count, pair_width)
    key_rows_out = (
        grand_total[..., :HEAD_DIM].reshape(tokens, head_count * HEAD_DIM).astype(jnp.bfloat16)
    )
    value_rows_out = (
        grand_total[..., HEAD_DIM:].reshape(tokens, head_count * HEAD_DIM).astype(jnp.bfloat16)
    )
    return (rows_last(outputs), rows_last(grad_query), key_rows_out, value_rows_out)


WHOLE_ROWS = 4096
GROUP = 4
VMEM_BYTES = 32 * 1024 * 1024


def dot(left, right, left_dim, right_dim):
    return lax.dot_general(
        left,
        right,
        (((left_dim,), (right_dim,)), ((), ())),
        preferred_element_type=jnp.float32,
    )


def listed_rows(tokens):
    return -(-(tokens // BLOCK * RAND) // 16) * 16


def pack_kernel(rand_hbm, key_hbm, value_hbm, query_hbm, grad_hbm, packed_hbm, *scratch):
    *targets, listed, packed, sems, out_sems = scratch
    rand_ref, key_ref, value_ref, query_ref, grad_ref = targets
    tokens, width = key_ref.shape
    heads = width // HEAD_DIM
    slots = packed.shape[0]
    copies = [
        pltpu.make_async_copy(source, target, sems.at[i])
        for i, (source, target) in enumerate(
            zip((rand_hbm, key_hbm, value_hbm, query_hbm, grad_hbm), targets)
        )
    ]
    sends = [
        pltpu.make_async_copy(packed.at[slot], packed_hbm.at[slot], out_sems.at[slot])
        for slot in range(slots)
    ]
    for copy in copies:
        copy.start()
    listed[...] = jnp.zeros_like(listed)
    for slot in range(heads, slots):
        packed[slot] = jnp.zeros(packed.shape[1:], jnp.bfloat16)
        sends[slot].start()
    for copy in copies:
        copy.wait()
    for block in range(tokens // BLOCK):
        listed[block * RAND : (block + 1) * RAND, :heads] = rand_ref[block]
    entries = listed[...].astype(jnp.float32).astype(jnp.bfloat16)
    for head in range(heads):
        cols = slice(head * HEAD_DIM, (head + 1) * HEAD_DIM)
        packed[head, :tokens] = jnp.concatenate((key_ref[:, cols], value_ref[:, cols]), axis=1)
        packed[head, tokens : 2 * tokens] = jnp.concatenate(
            (query_ref[:, cols], grad_ref[:, cols]), axis=1
        )
        packed[head, 2 * tokens :] = entries
        sends[head].start()
    for send in sends:
        send.wait()


def unpack_kernel(packed_ref, attended_ref, query_ref, key_ref, value_ref):
    tokens, width = key_ref.shape
    for head in range(width // HEAD_DIM):
        cols = slice(head * HEAD_DIM, (head + 1) * HEAD_DIM)
        first, second = packed_ref[head, :tokens], packed_ref[head, tokens:]
        query_ref[:, cols] = first[:, :HEAD_DIM]
        attended_ref[:, cols] = first[:, HEAD_DIM:]
        key_ref[:, cols] = second[:, :HEAD_DIM]
        value_ref[:, cols] = second[:, HEAD_DIM:]


def places_kernel(pos_row_ref, pos_col_ref, pick_ref, spread_ref):
    position = lax.broadcasted_iota(jnp.int32, pick_ref.shape, 1)
    pick_ref[...] = (position == pos_col_ref[...]).astype(jnp.bfloat16)
    position = lax.broadcasted_iota(jnp.int32, spread_ref.shape, 0)
    spread_ref[...] = (position == pos_row_ref[...]).astype(jnp.bfloat16)


def attend_kernel(
    pick_ref, spread_ref, x_ref, out_ref, acc, global_kv, global_acc, listed, starts, sem
):
    shards = out_ref.shape[0]
    tokens = out_ref.shape[1] // 2
    stride = x_ref.shape[0] // shards
    blocks = tokens // BLOCK
    own = lax.axis_index("seq")

    lists = jnp.zeros(listed.shape, jnp.float32)
    list_lane = lax.broadcasted_iota(jnp.int32, listed.shape, 1)
    for shard in range(shards):
        row = x_ref[shard * stride + 2 * tokens : (shard + 1) * stride].astype(jnp.float32)
        entry = jnp.sum(jnp.where(list_lane == own, row, 0.0), axis=1, keepdims=True)
        lists = jnp.where(list_lane == shard, entry, lists)
    passed = jnp.floor((lists + 0.5) * (1.0 / blocks))
    listed[...] = (lists * BLOCK + passed * (stride - tokens)).astype(jnp.int32)
    copy = pltpu.make_async_copy(listed, starts, sem)
    copy.start()
    for shard in range(shards):
        acc[shard * stride : shard * stride + tokens] = jnp.zeros(
            (tokens, 2 * HEAD_DIM), jnp.float32
        )
    global_acc[...] = jnp.zeros_like(global_acc)
    all_kv = jnp.concatenate(
        [x_ref[shard * stride : shard * stride + tokens] for shard in range(shards)], axis=0
    )
    global_kv[...] = dot(pick_ref[...], all_kv, 1, 0).astype(jnp.bfloat16)
    copy.wait()
    lane = lax.broadcasted_iota(jnp.int32, (BLOCK, 6 * BLOCK), 1)
    half = lax.broadcasted_iota(jnp.int32, (BLOCK, 2 * HEAD_DIM), 1) < HEAD_DIM
    query_mask = jnp.where(half, 1.0 / math.sqrt(HEAD_DIM), 0.0).astype(jnp.bfloat16)
    grad_mask = jnp.where(half, 0.0, 1.0).astype(jnp.bfloat16)

    def at(start):
        return pl.ds(pl.multiple_of(start, 16), BLOCK)

    def products(shard):
        base = shard * stride
        rows = []
        for block in range(blocks):
            rest = x_ref[at(base + tokens + block * BLOCK)]
            rows += [rest * query_mask, rest * grad_mask]
        rows = jnp.concatenate(rows, axis=0)
        all_places, local_kvs, local_dots = [], [], []
        for block in range(blocks):
            before = jnp.maximum(shard - 1, 0) * stride + (blocks - 1) * BLOCK
            after = jnp.minimum(shard + 1, shards - 1) * stride
            places = [
                base + (block - 1) * BLOCK if block else before,
                base + block * BLOCK,
                base + (block + 1) * BLOCK if block < blocks - 1 else after,
            ] + [starts[block * RAND + r, shard] for r in range(RAND)]
            all_places.append([at(p) for p in places])
            local_kvs.append(jnp.concatenate([x_ref[p] for p in all_places[-1]], axis=0))
            both = rows[2 * block * BLOCK : 2 * (block + 1) * BLOCK]
            local_dots.append(dot(both, local_kvs[-1], 1, 1))
        return rows, all_places, local_kvs, local_dots, dot(rows, global_kv[...], 1, 1)

    def weigh(shard, block, local_dots, global_dots):
        score, dp = local_dots[:BLOCK], local_dots[BLOCK:]
        if block == 0:
            score = jnp.where((lane < BLOCK) & (shard == 0), MASKED, score)
        if block == blocks - 1:
            outside = (lane >= 2 * BLOCK) & (lane < 3 * BLOCK)
            score = jnp.where(outside & (shard == shards - 1), MASKED, score)
        global_score, global_dp = global_dots[:BLOCK], global_dots[BLOCK:]
        highest = jnp.maximum(
            jnp.max(score, axis=1, keepdims=True),
            jnp.max(global_score, axis=1, keepdims=True),
        )
        local_exp = jnp.exp(score - highest)
        global_exp = jnp.exp(global_score - highest)
        inverse = 1.0 / (
            jnp.sum(local_exp, axis=1, keepdims=True)
            + jnp.sum(global_exp, axis=1, keepdims=True)
        )
        local_wf = local_exp * inverse
        global_wf = global_exp * inverse
        local_weight = local_wf.astype(jnp.bfloat16)
        global_weight = global_wf.astype(jnp.bfloat16)
        delta = jnp.sum(local_wf * dp, axis=1, keepdims=True) + jnp.sum(
            global_wf * global_dp, axis=1, keepdims=True
        )
        local_ds = local_weight * (dp - delta).astype(jnp.bfloat16)
        global_ds = global_weight * (global_dp - delta).astype(jnp.bfloat16)
        return (
            jnp.concatenate((local_ds, local_weight), axis=0),
            jnp.concatenate((global_ds, global_weight), axis=0),
        )

    def shard_group(group, carry):
        members = [group * GROUP + i for i in range(GROUP)]
        made = [products(shard) for shard in members]
        sides = [
            [
                weigh(
                    shard,
                    block,
                    local_dots[block],
                    global_dots[2 * block * BLOCK : 2 * (block + 1) * BLOCK],
                )
                for block in range(blocks)
            ]
            for shard, (_, _, _, local_dots, global_dots) in zip(members, made)
        ]
        gkv = global_kv[...]
        for shard, side, (rows, all_places, local_kvs, _, _) in zip(members, sides, made):
            global_side = jnp.concatenate([pair[1] for pair in side], axis=0)
            global_result = dot(global_side, gkv, 1, 0)
            results, grads = [], []
            for block in range(blocks):
                span = slice(2 * block * BLOCK, 2 * (block + 1) * BLOCK)
                results.append(dot(side[block][0], local_kvs[block], 1, 0) + global_result[span])
                grads.append(dot(side[block][0], rows[span], 0, 0))
            global_acc[...] += dot(rows, global_side, 0, 0)
            for block in range(blocks):
                out_ref[shard, block * BLOCK : (block + 1) * BLOCK] = jnp.where(
                    half,
                    results[block][:BLOCK] * (1.0 / math.sqrt(HEAD_DIM)),
                    results[block][BLOCK:],
                ).astype(jnp.bfloat16)
                for i, spot in enumerate(all_places[block]):
                    acc[spot] += grads[block][i * BLOCK : (i + 1) * BLOCK]
        return carry

    lax.fori_loop(0, shards // GROUP, shard_group, 0)
    global_grad = global_acc[...].astype(jnp.bfloat16)
    for shard in range(shards):
        spread = spread_ref[shard * tokens : (shard + 1) * tokens]
        out_ref[shard, tokens:] = (
            acc[shard * stride : shard * stride + tokens] + dot(spread, global_grad, 1, 1)
        ).astype(jnp.bfloat16)


def attend(whole, global_pos, tokens):
    shards, stride, pair = whole.shape
    lists = (stride - 2 * tokens, pair)
    global_count = global_pos.shape[0]
    pick, spread = pl.pallas_call(
        places_kernel,
        out_shape=(
            jax.ShapeDtypeStruct((global_count, shards * tokens), jnp.bfloat16),
            jax.ShapeDtypeStruct((shards * tokens, global_count), jnp.bfloat16),
        ),
        compiler_params=pltpu.CompilerParams(vmem_limit_bytes=VMEM_BYTES),
        cost_estimate=pl.CostEstimate(
            flops=4 * shards * tokens * global_count,
            bytes_accessed=4 * shards * tokens * global_count,
            transcendentals=0,
        ),
    )(global_pos.reshape(1, -1), global_pos.reshape(-1, 1))
    return pl.pallas_call(
        attend_kernel,
        out_shape=jax.ShapeDtypeStruct((shards, 2 * tokens, pair), jnp.bfloat16),
        scratch_shapes=[
            pltpu.VMEM((shards * stride, pair), jnp.float32),
            pltpu.VMEM((global_count, pair), jnp.bfloat16),
            pltpu.VMEM((pair, global_count), jnp.float32),
            pltpu.VMEM(lists, jnp.int32),
            pltpu.SMEM(lists, jnp.int32),
            pltpu.SemaphoreType.DMA,
        ],
        compiler_params=pltpu.CompilerParams(vmem_limit_bytes=VMEM_BYTES),
    )(pick, spread, whole.reshape(shards * stride, pair))


def whole_body(queries, key_input, value_input, grad_output, rand_blocks, global_pos):
    tokens, width = queries.shape
    shards = lax.axis_size("seq")
    extra = listed_rows(tokens)
    pair = 2 * HEAD_DIM
    slots = (shards, 2 * tokens + extra, pair)
    narrow = jax.ShapeDtypeStruct((tokens, width), jnp.bfloat16)
    anywhere = pl.BlockSpec(memory_space=pl.ANY)
    rand_lists = rand_blocks.transpose(0, 2, 1)
    packed = pl.pallas_call(
        pack_kernel,
        out_shape=jax.ShapeDtypeStruct(slots, jnp.bfloat16),
        in_specs=[anywhere] * 5,
        out_specs=anywhere,
        scratch_shapes=[pltpu.VMEM(rand_lists.shape, jnp.int32)]
        + [pltpu.VMEM((tokens, width), jnp.bfloat16)] * 4
        + [
            pltpu.VMEM((extra, pair), jnp.int32),
            pltpu.VMEM(slots, jnp.bfloat16),
            pltpu.SemaphoreType.DMA((5,)),
            pltpu.SemaphoreType.DMA((shards,)),
        ],
    )(rand_lists, key_input, value_input, queries, grad_output)
    whole = lax.all_to_all(packed, "seq", split_axis=0, concat_axis=0, tiled=True)
    result = attend(whole, global_pos, tokens)
    returned = lax.all_to_all(result, "seq", split_axis=0, concat_axis=0, tiled=True)
    return pl.pallas_call(
        unpack_kernel,
        out_shape=(narrow,) * 4,
        compiler_params=pltpu.CompilerParams(vmem_limit_bytes=VMEM_BYTES),
    )(returned)


def body(queries, *others):
    shards = lax.axis_size("seq")
    tokens, width = queries.shape
    if width // HEAD_DIM <= shards and shards * tokens <= WHOLE_ROWS:
        return whole_body(queries, *others)
    return sparse_body(queries, *others)


def solution(mesh):
    in_specs = (
        P(("groups", "seq"), "head"),
        P(("groups", "seq"), "head"),
        P(("groups", "seq"), "head"),
        P(("groups", "seq"), "head"),
        P(("groups", "seq"), "head", None),
        P("groups"),
    )
    out_specs = (
        P(("groups", "seq"), "head"),
        P(("groups", "seq"), "head"),
        P(("groups", "seq"), "head"),
        P(("groups", "seq"), "head"),
    )
    return jax.shard_map(body, mesh=mesh, in_specs=in_specs, out_specs=out_specs, check_vma=False)
```
